128 devices in a mesh: front: 2 (over core), row: 4 (over y), col: 16 (over x, z).
Axes of the slice: x: 4, y: 4, z: 4, core: 2. Of those that a mesh axis runs over, the one named last changes fastest.
Arguments:
- child_fronts: float32 [4, 6144, 6144], P('front', 'row', 'col'), as said below
- parent_front: float32 [12288, 12288], P('row', ('front', 'col')), as said below
- child_inverses: float32 [4, 2, 128, 128], P('front'), as said below
- parent_inverses: float32 [5, 128, 128], replicated, as said below
- block_map: int32 [4, 48], P('front'), may hold values from -1 to 95, as said below
Outputs:
- parent_factor: float32 [12288, 12288], P('row', ('front', 'col'))
The draws below stay inside these ranges and needn't reach their ends.
Inputs may be any that keep to these rules, and one draw needn't show every extreme that they name: `child_fronts`: each child front is symmetric in logical order. `parent_front`: the parent front is symmetric in logical order. `child_inverses`: every block is symmetric. `parent_inverses`: every block is symmetric. `block_map`: entry [c, j] is -1 exactly for the pivot blocks j < 2; otherwise it is the parent block that child block j of child c is added into. Child c belongs to front group g = c // 2, and its blocks land on parent blocks p with p % 32 between g * 16 and g * 16 + 15. Distinct blocks of one child land on distinct parent blocks. For each front group there is one offset per child of the group and per t = j // 16 such that block j lands on a parent block congruent to j plus that offset modulo 16. Among the contribution blocks of the 2 children of a group with one value of j % 16, at most 1 land on parent blocks with one value of p % 16; among those with one value of j % 4, at most 8 land on parent blocks with one value of p % 4. Both bounds are reached in every draw.
All inputs are finite; a program needn't handle non-finite values.
Results may differ from the reference program's by a relative error of at most 0.0003.
Values sent between devices are 32-bit elements; how exact they have to be, the bound alone decides.
A program may use at most 256 MiB of HBM per device.

```python
import math
import jax
import jax.numpy as jnp
from jax import lax

B = 128
TCOL = 3
UCOL = 3
CPF = 2
KPB = 2
PPB = 5
PROWS = 4
PCOLS = 16
PGRID = 32
NKIDS = 4
NCB = 48
NCH = 6144
NPAR = 12288


def stored_order(logical, row_owners, col_owners, block_size):
    order_n = logical.shape[0]
    pieces = logical.reshape(order_n // (row_owners * block_size), row_owners, block_size, order_n // (col_owners * block_size), col_owners, block_size)
    return pieces.transpose(1, 0, 2, 4, 3, 5).reshape(order_n, order_n)


def symmetric_front(samples, diagonal):
    order_n = samples.shape[-1]
    mixed = (samples + jnp.swapaxes(samples, -1, -2)) * 0.70710678
    indices = jnp.arange(order_n)
    return mixed.at[..., indices, indices].add(diagonal)


def inverse_blocks(samples, diagonal):
    block_size = samples.shape[-1]
    mixed = (samples + jnp.swapaxes(samples, -1, -2)) * (0.35 / math.sqrt(block_size))
    identity = jnp.eye(block_size, dtype=jnp.float32)
    return (mixed + identity * diagonal[..., None]) * (0.27 / math.sqrt(block_size))


def draw_child_fronts(key, part):
    key = jax.random.fold_in(key, 11)
    first_key, second_key = jax.random.split(key)
    shape_all = (NKIDS, NCH, NCH)
    samples = jax.random.normal(first_key, shape_all, jnp.float32)
    diagonal = jax.random.uniform(second_key, (NKIDS, NCH), jnp.float32, 0.5, 1.5) * math.sqrt(B)
    logical = symmetric_front(samples, diagonal)
    return jax.vmap(lambda single: stored_order(single, PROWS, PCOLS, B))(logical)


def draw_parent_front(key, part):
    key = jax.random.fold_in(key, 12)
    first_key, second_key = jax.random.split(key)
    shape_all = (NPAR, NPAR)
    samples = jax.random.normal(first_key, shape_all, jnp.float32)
    diagonal = jax.random.uniform(second_key, (NPAR,), jnp.float32, 0.5, 1.5) * math.sqrt(B)
    return stored_order(symmetric_front(samples, diagonal), PROWS, PGRID, B)


def draw_child_inverses(key, part):
    key = jax.random.fold_in(key, 13)
    first_key, second_key = jax.random.split(key)
    shape_all = (NKIDS, KPB, B, B)
    samples = jax.random.normal(first_key, shape_all, jnp.float32)
    diagonal = jax.random.uniform(second_key, (NKIDS, KPB, B), jnp.float32, 0.5, 1.5)
    return inverse_blocks(samples, diagonal)


def draw_parent_inverses(key, part):
    key = jax.random.fold_in(key, 17)
    first_key, second_key = jax.random.split(key)
    shape_all = (PPB, B, B)
    samples = jax.random.normal(first_key, shape_all, jnp.float32)
    diagonal = jax.random.uniform(second_key, (PPB, B), jnp.float32, 0.5, 1.5)
    return inverse_blocks(samples, diagonal)


def draw_block_map(key, part):
    key = jax.random.fold_in(key, 19)
    keys = jax.random.split(key, 4)
    groups = NKIDS // CPF
    spread = CPF * TCOL
    copies = (spread + PCOLS - 1) // PCOLS
    total = PCOLS * copies
    fold_count = PCOLS // PROWS
    index_all = jnp.arange(total)
    values = index_all % PCOLS
    copy_number = index_all // PCOLS
    residue = values % PROWS
    within = values // PROWS
    scores = jax.random.randint(keys[0], (groups, PROWS, fold_count), 0, 1 << 20) * fold_count + jnp.arange(fold_count)
    within_rank = jnp.argsort(jnp.argsort(scores, axis=-1), axis=-1)
    rotation = jax.random.randint(keys[1], (groups, 1), 0, PROWS)
    ranking = copy_number[None, :] * fold_count + within_rank[:, residue, within]
    order_key = ranking * PROWS + (residue[None, :] - rotation) % PROWS
    ordered = jnp.argsort(order_key, axis=-1)
    chosen = jnp.take_along_axis(jnp.broadcast_to(values, (groups, total)), ordered, axis=-1)[:, :spread]
    shuffle_scores = jax.random.randint(keys[2], (groups, spread), 0, 1 << 20) * spread + jnp.arange(spread)
    offsets = jnp.take_along_axis(chosen, jnp.argsort(shuffle_scores, axis=-1), axis=-1)
    children = jnp.arange(NKIDS)
    group_of = children // CPF
    member = children % CPF
    blocks = jnp.arange(NCB)
    column_of = blocks % PCOLS
    slot_of = blocks // PCOLS
    chosen_offset = offsets[group_of[:, None], member[:, None] * TCOL + slot_of[None, :]]
    landing = (column_of[None, :] + chosen_offset) % PCOLS
    place_scores = jax.random.randint(keys[3], (NKIDS, PCOLS, UCOL), 0, 1 << 20) * UCOL + jnp.arange(UCOL)
    place_perm = jnp.argsort(place_scores, axis=-1)
    placed = place_perm[children[:, None], landing, slot_of[None, :]]
    target = PGRID * placed + group_of[:, None] * PCOLS + landing
    return jnp.where(blocks[None, :] < KPB, -1, target).astype(jnp.int32)


def setup_inputs(seed: int = 0) -> dict:
    key_of = jax.random.split(jax.random.key(seed), 6)
    return {
        "child_fronts": draw_child_fronts(jax.random.fold_in(key_of[5], 71), 0),
        "parent_front": draw_parent_front(jax.random.fold_in(key_of[5], 71), 0),
        "child_inverses": draw_child_inverses(jax.random.fold_in(key_of[5], 71), 0),
        "parent_inverses": draw_parent_inverses(jax.random.fold_in(key_of[5], 71), 0),
        "block_map": draw_block_map(jax.random.fold_in(key_of[5], 71), 0),
    }


HIGHEST = lax.Precision.HIGHEST


def product(first, second):
    return jnp.dot(first, second, precision=HIGHEST, preferred_element_type=jnp.float32)


def to_logical(stored, row_owners, col_owners):
    order_n = stored.shape[0]
    pieces = stored.reshape(row_owners, order_n // (row_owners * B), B, col_owners, order_n // (col_owners * B), B)
    return pieces.transpose(1, 0, 2, 4, 3, 5).reshape(order_n, order_n)


def to_stored(logical, row_owners, col_owners):
    order_n = logical.shape[0]
    pieces = logical.reshape(order_n // (row_owners * B), row_owners, B, order_n // (col_owners * B), col_owners, B)
    return pieces.transpose(1, 0, 2, 4, 3, 5).reshape(order_n, order_n)


def eliminate(matrix, inverses, count_steps):
    for pivot_step in range(count_steps):
        begin_at = pivot_step * B
        end_at = begin_at + B
        inverse = inverses[pivot_step]
        scaled_cols = product(matrix[end_at:, begin_at:end_at], inverse)
        row_panel = matrix[begin_at:end_at, end_at:]
        scaled_rows = product(inverse, row_panel)
        trailing = matrix[end_at:, end_at:] - product(scaled_cols, row_panel)
        matrix = matrix.at[end_at:, end_at:].set(trailing)
        matrix = matrix.at[end_at:, begin_at:end_at].set(scaled_cols)
        matrix = matrix.at[begin_at:end_at, end_at:].set(scaled_rows)
    return matrix


def reference(child_fronts, parent_front, child_inverses, parent_inverses, block_map):
    assembled = to_logical(parent_front, PROWS, PGRID)
    parent_blocks = NPAR // B
    count_blocks = NCB - KPB
    for kid_index in range(NKIDS):
        front_done = eliminate(to_logical(child_fronts[kid_index], PROWS, PCOLS), child_inverses[kid_index], KPB)
        targets = block_map[kid_index, KPB:].astype(jnp.int32)
        tile_grid = front_done[KPB * B:, KPB * B:].reshape(count_blocks, B, count_blocks, B).transpose(0, 2, 1, 3)
        block_grid = assembled.reshape(parent_blocks, B, parent_blocks, B).transpose(0, 2, 1, 3)
        block_grid = block_grid.at[targets[:, None], targets[None, :]].add(tile_grid)
        assembled = block_grid.transpose(0, 2, 1, 3).reshape(NPAR, NPAR)
    return to_stored(eliminate(assembled, parent_inverses, PPB), PROWS, PGRID)
```

```python
import functools

import jax
import jax.numpy as jnp
from jax import lax
from jax.experimental import pallas as pl
from jax.experimental.pallas import tpu as pltpu
from jax.sharding import PartitionSpec as P

MESH = pl.DeviceIdType.MESH
HIGHEST = lax.Precision.HIGHEST
F32 = jnp.float32
ANY = pl.BlockSpec(memory_space=pl.ANY)
VMEM = pl.BlockSpec(memory_space=pltpu.VMEM)
SMEM = pl.BlockSpec(memory_space=pltpu.SMEM)
B = 128
PIECE = 48


def dot(a, b):
    return jnp.dot(a, b, precision=HIGHEST, preferred_element_type=F32)


def place():
    col = lax.axis_index("col")
    return lax.axis_index("front"), lax.axis_index("row"), col // 4, col % 4


def ring(i, d):
    return lax.rem(i + d + 4, 4)


def gather_kernel(panels, locals_, cross, exchange, src_ref, u_ref, w_ref, pp_ref, loc, loct, *sems):
    (ls, su, ru, ss, rs, s2, r2, s3, r3, s4, r4, s5, r5) = sems
    f, y, x, z = place()
    count = len(panels)
    own = f if cross else 0

    loads = []
    for i, take in enumerate(locals_):
        cp = pltpu.make_async_copy(take(src_ref), loc.at[i], ls.at[i])
        cp.start()
        loads.append(cp)

    barrier = pltpu.get_barrier_semaphore()
    greeted = 0
    for dy in range(4):
        for dz in range(4):
            if dy or dz:
                pl.semaphore_signal(
                    barrier, inc=1, device_id=(f, ring(y, dy), 4 * x + ring(z, dz)), device_id_type=MESH
                )
                greeted += 1
    for dx in range(1, 4):
        pl.semaphore_signal(barrier, inc=1, device_id=(f, y, 4 * ring(x, dx) + z), device_id_type=MESH)
        greeted += 1
    if cross:
        pl.semaphore_signal(barrier, inc=1, device_id=(1 - f, y, 4 * x + z), device_id_type=MESH)
        greeted += 1
    for i, cp in enumerate(loads):
        cp.wait()
        for t in range(3):
            flat = loc[i, :, t * B : (t + 1) * B].T
            for n in range(8):
                lo, hi = max(n * PIECE, t * B), min((n + 1) * PIECE, (t + 1) * B)
                if lo < hi:
                    loct[i, n // 2, n % 2, lo - n * PIECE : hi - n * PIECE, :] = flat[lo - t * B : hi - t * B]
    pl.semaphore_wait(barrier, greeted)

    def remote(src, dst, ssem, rsem, device):
        return pltpu.make_async_remote_copy(
            src_ref=src, dst_ref=dst, send_sem=ssem, recv_sem=rsem, device_id=device, device_id_type=MESH
        )

    def first(p, op):
        sy, i = panels[p]
        for zz in range(4):
            mine = (y == z) & (z == zz)
            cp = remote(loct.at[i, zz], w_ref.at[own, p, x, zz], ss.at[p, zz], rs.at[p], (f, z, 4 * x + zz))
            here = pltpu.make_async_copy(loct.at[i, zz], w_ref.at[own, p, x, zz], ss.at[p, zz])

            @pl.when(jnp.logical_not(mine))
            def _():
                cp.start() if op == "start" else cp.wait_send()

            @pl.when(mine)
            def _():
                here.start() if op == "start" else here.wait()

        for dy in range(1, 4):
            cp = remote(loc.at[i], u_ref.at[p], su.at[p, dy], ru.at[p], (f, ring(y, dy), 4 * x + z))
            cp.start() if op == "start" else cp.wait_send()
        here = pltpu.make_async_copy(loc.at[i], u_ref.at[p], su.at[p, 0])
        here.start() if op == "start" else here.wait()

    for p, (sy, i) in enumerate(panels):
        pl.when(y == sy)(functools.partial(first, p, "start"))
    for p, (sy, i) in enumerate(panels):
        pl.when(y == sy)(functools.partial(first, p, "wait"))
    for p, (sy, i) in enumerate(panels):

        @pl.when(jnp.logical_not((y == sy) & (y == z)))
        def _():
            remote(w_ref.at[own, p, x, z], w_ref.at[own, p, x, z], ss.at[p, 0], rs.at[p], (f, y, 4 * x + z)).wait_recv()

    along_x = [w_ref.at[own, :, ring(x, -d), z, 0] for d in range(4)]
    along_z = [w_ref.at[own, :, x, ring(z, -d), 1] for d in range(4)]
    sent = []
    for d in (1, 3, 2):
        cp = remote(along_x[0], along_x[0], s2.at[0, d], r2.at[0, d], (f, y, 4 * ring(x, d) + z))
        cp.start()
        sent.append(cp)
        cp = remote(along_z[0], along_z[0], s2.at[1, d], r2.at[1, d], (f, y, 4 * x + ring(z, d)))
        cp.start()
        sent.append(cp)

    def arrived(region, rsem):
        remote(region, region, s2.at[0, 0], rsem, (f, y, 4 * x + z)).wait_recv()

    other = (1 - f, y, 4 * x + z)

    def across(n, region):
        if cross:
            cp = remote(region, region, s4.at[n], r4.at[n], other)
            cp.start()
            sent.append(cp)

    for d in (1, 3, 2):
        arrived(along_x[d], r2.at[0, d])
    part_x = [w_ref.at[own, :, :, ring(z, -d), 0] for d in range(4)]
    for d in (1, 3, 2):
        cp = remote(part_x[0], part_x[0], s3.at[0, d], r3.at[0, d], (f, y, 4 * x + ring(z, d)))
        cp.start()
        sent.append(cp)
    for d in (1, 3, 2):
        arrived(along_z[d], r2.at[1, d])
    part_z = [w_ref.at[own, :, ring(x, -d), :, 1] for d in range(4)]
    for d in (1, 3, 2):
        cp = remote(part_z[0], part_z[0], s3.at[1, d], r3.at[1, d], (f, y, 4 * ring(x, d) + z))
        cp.start()
        sent.append(cp)
    across(0, part_x[0])
    across(4, part_z[0])
    for d in (1, 3, 2):
        arrived(part_x[d], r3.at[0, d])
        across(d, part_x[d])
        arrived(part_z[d], r3.at[1, d])
        across(4 + d, part_z[d])
    if cross:
        theirs_x = [w_ref.at[1 - f, :, :, ring(z, -d), 0] for d in range(4)]
        theirs_z = [w_ref.at[1 - f, :, ring(x, -d), :, 1] for d in range(4)]
        for d in range(4):
            arrived(theirs_x[d], r4.at[d])
            arrived(theirs_z[d], r4.at[4 + d])

    def couple(e, op):
        sy, base, n, m = exchange[e]
        for part, (src, dst) in enumerate(
            (
                (w_ref.at[0, 0:n, m, 0], pp_ref.at[base : base + n, 0:2]),
                (w_ref.at[0, 0:n, m, 1, 0], pp_ref.at[base : base + n, 2]),
            )
        ):
            for dy in range(1, 4):
                cp = remote(src, dst, s5.at[e, part, dy], r5.at[e, part], (f, ring(y, dy), 4 * x + z))
                cp.start() if op == "start" else cp.wait_send()
            cp = pltpu.make_async_copy(src, dst, s5.at[e, part, 0])
            cp.start() if op == "start" else cp.wait()

    for e, (sy, base, n, m) in enumerate(exchange):
        pl.when(y == sy)(functools.partial(couple, e, "start"))
    for e, (sy, base, n, m) in enumerate(exchange):

        @pl.when(y != sy)
        def _():
            arrived(pp_ref.at[base : base + n, 0:2], r5.at[e, 0])
            arrived(pp_ref.at[base : base + n, 2], r5.at[e, 1])

        pl.when(y == sy)(functools.partial(couple, e, "wait"))
    for p, (sy, i) in enumerate(panels):

        @pl.when(y != sy)
        def _():
            arrived(u_ref.at[p], ru.at[p])

    for cp in sent:
        cp.wait_send()


def gather(source, panels, locals_, cross, exchange, pairs, cid):
    count, fronts = len(panels), 2 if cross else 1
    dma = pltpu.SemaphoreType.DMA
    n = len(locals_)

    def kernel(src_ref, u_ref, w_ref, pp_ref, loc, loct, *sems):
        gather_kernel(panels, locals_, cross, exchange, src_ref, u_ref, w_ref, pp_ref, loc, loct, *sems)

    u, w, pp = pl.pallas_call(
        kernel,
        out_shape=(
            jax.ShapeDtypeStruct((count, B, 3 * B), F32),
            jax.ShapeDtypeStruct((fronts, count, 4, 4, 2, PIECE, B), F32),
            jax.ShapeDtypeStruct((pairs, 3, PIECE, B), F32),
        ),
        in_specs=[ANY],
        out_specs=(ANY, ANY, ANY),
        scratch_shapes=[
            pltpu.VMEM((n, B, 3 * B), F32),
            pltpu.VMEM((n, 4, 2, PIECE, B), F32),
            dma((n,)),
            dma((count, 4)),
            dma((count,)),
            dma((count, 4)),
            dma((count,)),
            dma((2, 4)),
            dma((2, 4)),
            dma((2, 4)),
            dma((2, 4)),
            dma((8,)),
            dma((8,)),
            dma((len(exchange), 2, 4)),
            dma((len(exchange), 2)),
        ],
        compiler_params=pltpu.CompilerParams(
            collective_id=cid, has_side_effects=True, vmem_limit_bytes=16 << 20
        ),
        name="gather_panels",
    )(source)
    return u, w.reshape(fronts, count, 4, 3 * B, B), pp.reshape(pairs, 3 * PIECE, B)


def offsets(map_ref):
    return [lax.rem(map_ref[c, 16 * t + 3] - 3 + 16, 16) for c in range(2) for t in range(3)]


def slots(offs):
    table = {}
    for r in range(4):
        first, second = jnp.int32(-1), jnp.int32(-1)
        for i, o in enumerate(offs):
            hit = lax.rem(o, 4) == r
            second = jnp.where(hit & (first >= 0), i, second)
            first = jnp.where(hit & (first < 0), i, first)
        table[r, 0], table[r, 1] = first, second
    return table


def pick(values, index):
    out = values[0]
    for i in range(1, len(values)):
        out = jnp.where(index == i, values[i], out)
    return out


def child_kernel(map_ref, f_ref, u_ref, w_ref, pp_ref, g_ref, out_ref, q_ref, l_ref):
    f, y, x, z = place()
    offs = offsets(map_ref)
    for c in range(2):
        l10 = dot(pp_ref[c, 0:B, :], g_ref[c, 0])
        l_ref[c] = l10.T
        v0 = u_ref[c]
        v1 = u_ref[2 + c] - dot(l10, v0)
        q_ref[c, 0:B, :] = dot(g_ref[c, 0], v0)
        q_ref[c, B : 2 * B, :] = dot(g_ref[c, 1], v1)
    for i in range(6):
        c, t = i // 3, i % 3
        r, q = lax.rem(offs[i], 4), offs[i] // 4
        rank = jnp.int32(0)
        for k in range(i):
            rank = rank + (lax.rem(offs[k], 4) == r).astype(jnp.int32)
        carry = (y + r) // 4
        dz = ring(lax.rem(y + r, 4), -z)

        def slab(m, _, c=c, t=t, q=q, rank=rank, carry=carry, dz=dz):
            dx = ring(lax.rem(m + q + carry, 4), -x)
            rows = pl.ds(t * B, B)
            w0 = w_ref[0, c, m, rows, :]
            w1 = w_ref[0, 2 + c, m, rows, :] - dot(w0, l_ref[c])
            full = jnp.concatenate([w0, w1], axis=1)
            out_ref[dz, rank, dx] = f_ref[c, 4 * t + m] - dot(full, q_ref[c])
            return 0

        lax.fori_loop(0, 4, slab, 0)


def child_update(block_map, fronts, u, w, pp, inverses):
    return pl.pallas_call(
        child_kernel,
        out_shape=jax.ShapeDtypeStruct((4, 2, 4, B, 3 * B), F32),
        in_specs=[SMEM, VMEM, VMEM, VMEM, VMEM, VMEM],
        out_specs=VMEM,
        scratch_shapes=[pltpu.VMEM((2, 2 * B, 3 * B), F32), pltpu.VMEM((2, B, B), F32)],
        compiler_params=pltpu.CompilerParams(vmem_limit_bytes=48 << 20),
        name="child_update",
    )(block_map, fronts.reshape(2, 12, B, 3 * B), u, w, pp, inverses)


def exchange_kernel(map_ref, in_ref, out_ref, rz, rx, sy, *sems):
    szs, szr, sxs, sxr, sys_, syr, own_sem = sems
    f, y, x, z = place()

    barrier = pltpu.get_barrier_semaphore()
    for d in range(1, 4):
        for device in (
            (f, ring(y, d), 4 * x + z),
            (f, y, 4 * ring(x, d) + z),
            (f, y, 4 * x + ring(z, d)),
        ):
            pl.semaphore_signal(barrier, inc=1, device_id=device, device_id_type=MESH)
    own = pltpu.make_async_copy(in_ref.at[0], rz.at[0], own_sem)
    own.start()
    pl.semaphore_wait(barrier, 9)

    offs = offsets(map_ref)
    table = slots(offs)
    residues = [lax.rem(o, 4) for o in offs]

    def remote(src, dst, ssem, rsem, device):
        return pltpu.make_async_remote_copy(
            src_ref=src, dst_ref=dst, send_sem=ssem, recv_sem=rsem, device_id=device, device_id_type=MESH
        )

    def z_copy(dz, s, dx):
        return remote(
            in_ref.at[dz, s, dx], rz.at[dz, s, dx], szs.at[dz, s, dx], szr.at[dz, s, dx], (f, y, 4 * x + ring(z, dz))
        )

    def x_copy(dx, dz, s):
        return remote(
            rz.at[dz, s, dx], rx.at[dx, dz, s], sxs.at[dx, dz, s], sxr.at[dx, dz, s], (f, y, 4 * ring(x, dx) + z)
        )

    def y_copy(dy, s, dx):
        return remote(
            sy.at[dy, s, dx], out_ref.at[dy, s, dx], sys_.at[dy, s, dx], syr.at[dy, s, dx], (f, ring(y, dy), 4 * x + z)
        )

    groups = [(s, dx) for s in range(2) for dx in (1, 3, 2, 0)]
    for s, dx in groups:
        for dz in (1, 3, 2):
            z_copy(dz, s, dx).start()
    own.wait()

    def pass_x(s, dx):
        for dz in (0, 1, 3, 2):
            if dz:
                z_copy(dz, s, dx).wait_recv()
            if dx:
                x_copy(dx, dz, s).start()

    def pass_y(s, dx):
        if dx:
            for dz in range(4):
                x_copy(dx, dz, s).wait_recv()
        home = ring(z, -y)
        slot = pick([table[r, s] for r in range(4)], home)
        for dy in (1, 3, 2, 0):
            for t in range(3):
                res = jnp.where(slot >= 3, residues[3 + t], residues[t])
                origin = lax.rem(ring(y, dy) - res + 4, 4)
                dz = lax.rem(z - origin + 4, 4)
                lanes = slice(t * B, (t + 1) * B)
                if dx:
                    cands = [rx[dx, k, s, :, lanes] for k in range(4)]
                else:
                    cands = [rz[k, s, 0, :, lanes] for k in range(4)]
                sy[dy, s, dx, :, lanes] = pick(cands, dz)
            if dy:
                y_copy(dy, s, dx).start()
            else:
                pltpu.make_async_copy(sy.at[0, s, dx], out_ref.at[0, s, dx], sys_.at[0, s, dx]).start()

    for n in range(len(groups) + 1):
        if n < len(groups):
            pass_x(*groups[n])
        if n:
            pass_y(*groups[n - 1])
    for s, dx in groups:
        for d in (1, 3, 2):
            z_copy(d, s, dx).wait_send()
            y_copy(d, s, dx).wait_send()
        if dx:
            for dz in range(4):
                x_copy(dx, dz, s).wait_send()
        pltpu.make_async_copy(sy.at[0, s, dx], out_ref.at[0, s, dx], sys_.at[0, s, dx]).wait()
        for d in (1, 3, 2):
            y_copy(d, s, dx).wait_recv()


def exchange(block_map, staged, cid):
    dma = pltpu.SemaphoreType.DMA
    slab = (B, 3 * B)
    return pl.pallas_call(
        exchange_kernel,
        out_shape=jax.ShapeDtypeStruct((4, 2, 4) + slab, F32),
        in_specs=[SMEM, ANY],
        out_specs=ANY,
        scratch_shapes=[
            pltpu.VMEM((4, 2, 4) + slab, F32),
            pltpu.VMEM((4, 4, 2) + slab, F32),
            pltpu.VMEM((4, 2, 4) + slab, F32),
            dma((4, 2, 4)),
            dma((4, 2, 4)),
            dma((4, 4, 2)),
            dma((4, 4, 2)),
            dma((4, 2, 4)),
            dma((4, 2, 4)),
            dma,
        ],
        compiler_params=pltpu.CompilerParams(
            collective_id=cid, has_side_effects=True, vmem_limit_bytes=40 << 20
        ),
        name="exchange",
    )(block_map, staged)


def extend_add(block_map, received, parent):
    def kernel(map_ref, in_ref, parent_ref, out_ref, acc):
        def load(u, _):
            for v in range(3):
                acc[u, v] = parent_ref[u, :, v * B : (v + 1) * B]
            return 0

        lax.fori_loop(0, 24, load, 0)
        add_body(map_ref, in_ref, acc)

        def store(u, _):
            for v in range(3):
                out_ref[u, :, v * B : (v + 1) * B] = acc[u, v]
            return 0

        lax.fori_loop(0, 24, store, 0)

    out = pl.pallas_call(
        kernel,
        out_shape=jax.ShapeDtypeStruct((24, B, 3 * B), F32),
        in_specs=[SMEM, VMEM, VMEM],
        out_specs=VMEM,
        scratch_shapes=[pltpu.VMEM((24, 3, B, B), F32)],
        compiler_params=pltpu.CompilerParams(vmem_limit_bytes=48 << 20),
        name="extend_add",
    )(block_map, received, parent.reshape(24, B, 3 * B))
    return out.reshape(24 * B, 3 * B)


def add_body(map_ref, in_ref, acc):
    f, y, x, z = place()
    offs = offsets(map_ref)
    table = slots(offs)
    for dy in range(4):
        src_y = ring(y, -dy)
        r = ring(z, -src_y)
        carry = (src_y + r) // 4
        for s in range(2):
            slot = pick([table[k, s] for k in range(4)], r)
            c = (slot >= 3).astype(jnp.int32)
            t_i = jnp.maximum(slot - 3 * c, 0)
            m = lax.rem(x - pick(offs, slot) // 4 - carry + 8, 4)
            i = 16 * t_i + 4 * m + src_y
            col_slot = map_ref[c, i] // 32
            for t in range(3):
                res = lax.rem(jnp.where(slot >= 3, offs[3 + t], offs[t]), 4)

                def step(dx, _, t=t, res=res, slot=slot, c=c, i=i, col_slot=col_slot, dy=dy, s=s):
                    j = 16 * t + 4 * ring(x, -dx) + ring(y, -res)
                    row_slot = map_ref[c, j] // 4

                    @pl.when((slot >= 0) & (i >= 2) & (j >= 2))
                    def _():
                        acc[row_slot, col_slot] += in_ref[dy, s, dx, :, t * B : (t + 1) * B].T

                    return 0

                lax.fori_loop(0, 4, step, 0)


PAIR = {(1, 0): 0, (2, 0): 1, (2, 1): 2, (3, 0): 3, (3, 1): 4, (3, 2): 5, (4, 0): 6, (4, 1): 7, (4, 2): 8, (4, 3): 9}


def parent_kernel(a_ref, u_ref, w_ref, pp_ref, g_ref, out_ref, cur, lt, v_ref, q_ref, wt):
    f, y, x, z = place()
    steps = range(5)
    for n in range(10):
        cur[n] = pp_ref[n, 0:B, :]
    for j in steps:
        v_ref[j] = u_ref[j]
    for j in range(4):
        for k in range(j + 1, 5):
            l_kj = dot(cur[PAIR[k, j]], g_ref[j])
            lt[PAIR[k, j]] = l_kj.T
            for i in range(j + 1, k):
                cur[PAIR[k, i]] -= dot(l_kj, cur[PAIR[i, j]].T)
            v_ref[k] -= dot(l_kj, v_ref[j])
    for k in steps:
        q_ref[k * B : (k + 1) * B, :] = dot(g_ref[k], v_ref[k])

    col = 4 * x + z
    pivot_col = (f == 0) & (col < 5)

    def rows(n, _):
        u, rest = n // 8, lax.rem(n, 8)
        ff, m = rest // 4, lax.rem(rest, 4)
        part = pl.ds(pl.multiple_of(u * B, B), B)
        for k in steps:
            w = w_ref[ff, k, m, part, :]
            if k:
                w = w - dot(
                    wt[:, 0 : k * B],
                    jnp.concatenate([lt[PAIR[k, j]] for j in range(k)], axis=0),
                )
            wt[:, k * B : (k + 1) * B] = w
        out_ref[n] = a_ref[n] - dot(wt[...], q_ref[...])

        @pl.when(pivot_col)
        def _():
            row = 4 * n + y
            for k in steps:

                @pl.when((col == k) & (row > k))
                def _():
                    out_ref[n, :, 0:B] = dot(wt[:, k * B : (k + 1) * B], g_ref[k])

                @pl.when((col == k) & (row == k))
                def _():
                    if k:
                        out_ref[n, :, 0:B] = a_ref[n, :, 0:B] - dot(wt[:, 0 : k * B], q_ref[0 : k * B, 0:B])
                    else:
                        out_ref[n, :, 0:B] = a_ref[n, :, 0:B]

        return 0

    lax.fori_loop(0, 24, rows, 0)
    for k in steps:

        @pl.when(y == k % 4)
        def _():
            panel = q_ref[k * B : (k + 1) * B, :]
            keep = (f == 0) & (col <= k)
            out_ref[k // 4, :, B:] = panel[:, B:]
            out_ref[k // 4, :, 0:B] = jnp.where(keep, out_ref[k // 4, :, 0:B], panel[:, 0:B])


def parent_update(a, u, w, pp, inverses):
    out = pl.pallas_call(
        parent_kernel,
        out_shape=jax.ShapeDtypeStruct((24, B, 3 * B), F32),
        in_specs=[VMEM] * 5,
        out_specs=VMEM,
        scratch_shapes=[
            pltpu.VMEM((10, B, B), F32),
            pltpu.VMEM((10, B, B), F32),
            pltpu.VMEM((5, B, 3 * B), F32),
            pltpu.VMEM((5 * B, 3 * B), F32),
            pltpu.VMEM((B, 5 * B), F32),
        ],
        compiler_params=pltpu.CompilerParams(vmem_limit_bytes=48 << 20),
        name="parent_update",
    )(a.reshape(24, B, 3 * B), u, w, pp, inverses)
    return out.reshape(24 * B, 3 * B)


CHILD_PANELS = ((0, 0), (0, 1), (1, 0), (1, 1))
PARENT_PANELS = ((0, 0), (1, 0), (2, 0), (3, 0), (0, 1))


def body(child_fronts, parent_front, child_inverses, parent_inverses, block_map):
    u, w, pp = gather(
        child_fronts,
        CHILD_PANELS,
        [lambda ref: ref.at[0, 0:B, :], lambda ref: ref.at[1, 0:B, :]],
        False,
        ((1, 0, 2, 0),),
        2,
        0,
    )
    staged = child_update(block_map, child_fronts, u, w, pp, child_inverses)
    received = exchange(block_map, staged, 1)
    a = extend_add(block_map, received, parent_front)
    u, w, pp = gather(
        a,
        PARENT_PANELS,
        [lambda ref: ref.at[0:B, :], lambda ref: ref.at[B : 2 * B, :]],
        True,
        ((1, 0, 1, 0), (2, 1, 2, 0), (3, 3, 3, 0), (0, 6, 4, 1)),
        10,
        2,
    )
    return parent_update(a, u, w, pp, parent_inverses)


def solution(mesh):
    placed = (
        P("front", "row", "col"),
        P("row", ("front", "col")),
        P("front", None, None, None),
        P(),
        P("front", None),
    )
    return jax.shard_map(
        body, mesh=mesh, in_specs=placed, out_specs=P("row", ("front", "col")), check_vma=False
    )
```

```python
import functools

import jax
import jax.numpy as jnp
from jax import lax
from jax.experimental import pallas as pl
from jax.experimental.pallas import tpu as pltpu
from jax.sharding import PartitionSpec as P

MESH = pl.DeviceIdType.MESH
F32, BF16 = jnp.float32, jnp.bfloat16
ANY = pl.BlockSpec(memory_space=pltpu.HBM)
VMEM = pl.BlockSpec(memory_space=pltpu.VMEM)
SMEM = pl.BlockSpec(memory_space=pltpu.SMEM)
DMA = pltpu.SemaphoreType.DMA
B = 128
AROUND = (1, 3, 2)
TILE = (4, 2, 16, B)


def split(a):
    high = a.astype(BF16)
    return high, (a - high.astype(F32)).astype(BF16)


def lhs3(a):
    high, low = split(a)
    return jnp.concatenate([high, high, low], axis=1)


def rhs3(b):
    high, low = split(b)
    return jnp.concatenate([high, low, high], axis=0)


def mul3(a, b):
    return jnp.dot(a, b, preferred_element_type=F32)


def dot(a, b):
    return mul3(lhs3(a), rhs3(b))


def place():
    col = lax.axis_index("col")
    return lax.axis_index("front"), lax.axis_index("row"), col // 4, col % 4


def ring(i, d):
    return lax.rem(i + d + 4, 4)


def remote(src, dst, ssem, rsem, device):
    return pltpu.make_async_remote_copy(
        src_ref=src, dst_ref=dst, send_sem=ssem, recv_sem=rsem, device_id=device, device_id_type=MESH
    )


def pick(values, index):
    out = values[0]
    for i in range(1, len(values)):
        out = jnp.where(index == i, values[i], out)
    return out


def gather(panels, cross, couplings, loc, loct, u_ref, w_ref, pp_ref, sems, idle):
    su, ru, ss, rs, s2, r2, s3, r3, s4, r4, s5, r5 = sems
    f, y, x, z = place()
    own = f if cross else 0
    late = []

    def scatter(p, op):
        i = panels[p][1]
        for zz in range(4):
            mine = (y == z) & (z == zz)
            src, dst = loct.at[i, :, zz], w_ref.at[own, p, x, :, zz]
            cp = remote(src, dst, ss.at[p, zz], rs.at[p], (f, z, 4 * x + zz))
            here = pltpu.make_async_copy(src, dst, ss.at[p, zz])

            @pl.when(jnp.logical_not(mine))
            def _():
                cp.start() if op == "start" else cp.wait_send()

            @pl.when(mine)
            def _():
                here.start() if op == "start" else here.wait()

    def column(p, op):
        i = panels[p][1]
        for dy in AROUND:
            cp = remote(loc.at[i], u_ref.at[p], su.at[p, dy], ru.at[p], (f, ring(y, dy), 4 * x + z))
            cp.start() if op == "start" else cp.wait_send()
        here = pltpu.make_async_copy(loc.at[i], u_ref.at[p], su.at[p, 0])
        here.start() if op == "start" else here.wait()

    for step in (scatter, column):
        for p, (sy, i) in enumerate(panels):
            pl.when(y == sy)(functools.partial(step, p, "start"))
    idle(0)
    for p, (sy, i) in enumerate(panels):
        region = w_ref.at[own, p, x, :, z]

        @pl.when(jnp.logical_not((y == sy) & (y == z)))
        def _():
            remote(region, region, ss.at[p, 0], rs.at[p], (f, y, 4 * x + z)).wait_recv()

        @pl.when((y == sy) & (y == z))
        def _():
            for zz in range(4):

                @pl.when(z == zz)
                def _():
                    pltpu.make_async_copy(region, region, ss.at[p, zz]).wait()

    along_x = [w_ref.at[own, :, ring(x, -d), :, z, 0] for d in range(4)]
    along_z = [w_ref.at[own, :, x, :, ring(z, -d), 1] for d in range(4)]
    part_x = [w_ref.at[own, :, :, :, ring(z, -d), 0] for d in range(4)]
    part_z = [w_ref.at[own, :, ring(x, -d), :, :, 1] for d in range(4)]

    def send(*args):
        cp = remote(*args)
        cp.start()
        late.append(cp)

    def arrived(region, rsem):
        remote(region, region, s2.at[0, 0], rsem, (f, y, 4 * x + z)).wait_recv()

    def across(n, region):
        if cross:
            send(region, region, s4.at[n], r4.at[n], (1 - f, y, 4 * x + z))

    for d in AROUND:
        send(along_x[0], along_x[0], s2.at[0, d], r2.at[0, d], (f, y, 4 * ring(x, d) + z))
        send(along_z[0], along_z[0], s2.at[1, d], r2.at[1, d], (f, y, 4 * x + ring(z, d)))
    idle(1)
    for d in AROUND:
        arrived(along_x[d], r2.at[0, d])
    for d in AROUND:
        send(part_x[0], part_x[0], s3.at[0, d], r3.at[0, d], (f, y, 4 * x + ring(z, d)))
    for d in AROUND:
        arrived(along_z[d], r2.at[1, d])
    for d in AROUND:
        send(part_z[0], part_z[0], s3.at[1, d], r3.at[1, d], (f, y, 4 * ring(x, d) + z))
    across(0, part_x[0])
    across(4, part_z[0])
    idle(2)
    for n, d in enumerate(AROUND):
        arrived(part_x[d], r3.at[0, d])
        across(d, part_x[d])
        arrived(part_z[d], r3.at[1, d])
        across(4 + d, part_z[d])
    if cross:
        for d in range(4):
            arrived(w_ref.at[1 - f, :, :, :, ring(z, -d), 0], r4.at[d])
            arrived(w_ref.at[1 - f, :, ring(x, -d), :, :, 1], r4.at[4 + d])

    def couple(e, op):
        sy, base, n, m = couplings[e]
        src, dst = w_ref.at[0, 0:n, m, 0], pp_ref.at[base : base + n]
        for dy in AROUND:
            cp = remote(src, dst, s5.at[e, dy], r5.at[e], (f, ring(y, dy), 4 * x + z))
            cp.start() if op == "start" else cp.wait_send()
        here = pltpu.make_async_copy(src, dst, s5.at[e, 0])
        here.start() if op == "start" else here.wait()

    for e, (sy, base, n, m) in enumerate(couplings):
        pl.when(y == sy)(functools.partial(couple, e, "start"))
    for p, (sy, i) in enumerate(panels):

        @pl.when(y != sy)
        def _():
            arrived(u_ref.at[p], ru.at[p])

    for e, (sy, base, n, m) in enumerate(couplings):

        @pl.when(y != sy)
        def _():
            arrived(pp_ref.at[base : base + n], r5.at[e])

        pl.when(y == sy)(functools.partial(couple, e, "wait"))

    def finish():
        def scatter_rest(p):
            i = panels[p][1]
            for zz in range(4):

                @pl.when(jnp.logical_not((y == z) & (z == zz)))
                def _():
                    src, dst = loct.at[i, :, zz], w_ref.at[own, p, x, :, zz]
                    remote(src, dst, ss.at[p, zz], rs.at[p], (f, z, 4 * x + zz)).wait_send()

        for p, (sy, i) in enumerate(panels):
            pl.when(y == sy)(functools.partial(scatter_rest, p))
        for cp in late:
            cp.wait_send()

    for p, (sy, i) in enumerate(panels):
        pl.when(y == sy)(functools.partial(column, p, "wait"))
    return finish


def gather_sems(count, couplings):
    return [
        DMA((count, 4)),
        DMA((count,)),
        DMA((count, 4)),
        DMA((count,)),
        DMA((2, 4)),
        DMA((2, 4)),
        DMA((2, 4)),
        DMA((2, 4)),
        DMA((8,)),
        DMA((8,)),
        DMA((couplings, 4)),
        DMA((couplings,)),
    ]


CHILD_PANELS = ((0, 0), (0, 1), (1, 0), (1, 1))
PARENT_PANELS = ((0, 0), (1, 0), (2, 0), (3, 0), (0, 1))
CHILD_COUPLINGS = ((1, 0, 2, 0),)
PARENT_COUPLINGS = ((1, 0, 1, 0), (2, 1, 2, 0), (3, 3, 3, 0), (0, 6, 4, 1))
PAIR = {(1, 0): 0, (2, 0): 1, (2, 1): 2, (3, 0): 3, (3, 1): 4, (3, 2): 5, (4, 0): 6, (4, 1): 7, (4, 2): 8, (4, 3): 9}


def assemble_kernel(
    map_ref, child_ref, parent_ref, ginv_ref, a_ref, u2, w2, pp2,
    fr, acc, loct, u1, w1, pp1, lt, qcat, stg, hop, fin, sy, got, load_sem, h1s, h1r, h2s, h2r, ys, yr, *sems
):
    f, y, x, z = place()
    here = (f, y, 4 * x + z)

    loads = [
        pltpu.make_async_copy(child_ref.at[:, 0:1], fr.at[:, 0:1], load_sem.at[0]),
        pltpu.make_async_copy(child_ref.at[:, 1:12], fr.at[:, 1:12], load_sem.at[1]),
        pltpu.make_async_copy(parent_ref, acc, load_sem.at[2]),
    ]
    for cp in loads:
        cp.start()

    barrier = pltpu.get_barrier_semaphore()
    greeted = []
    for dy in range(4):
        for dz in range(4):
            if dy or dz:
                greeted.append((f, ring(y, dy), 4 * x + ring(z, dz)))
    for dx in range(1, 4):
        greeted.append((f, y, 4 * ring(x, dx) + z))
    greeted.append((1 - f, y, 4 * x + z))
    for device in greeted:
        pl.semaphore_signal(barrier, inc=1, device_id=device, device_id_type=MESH)

    def turned(block):
        return block.T.reshape(TILE)

    offs = [lax.rem(map_ref[c, 16 * t + 3] - 3 + 16, 16) for c in range(2) for t in range(3)]
    residues = [lax.rem(o, 4) for o in offs]
    ranks = []
    for i in range(6):
        rank = jnp.int32(0)
        for k in range(i):
            rank = rank + (residues[k] == residues[i]).astype(jnp.int32)
        ranks.append(rank)

    def slot_of(r, s):
        slot = jnp.int32(-1)
        for i in range(6):
            slot = jnp.where((residues[i] == r) & (ranks[i] == s), i, slot)
        return slot

    loads[0].wait()
    for c in range(2):
        for t in range(3):
            loct[c, t] = turned(fr[c, 0, :, t * B : (t + 1) * B])
    pl.semaphore_wait(barrier, len(greeted))

    first_rows = fr.at[:, 0]
    finish1 = gather(
        CHILD_PANELS, False, CHILD_COUPLINGS, first_rows, loct, u1, w1, pp1, sems[0:12], lambda n: None
    )

    for c in range(2):
        l10 = dot(pp1[c].reshape(B, B), ginv_ref[c, 0])
        lt[c] = rhs3(l10.T)
        v0 = u1[c]
        v1 = u1[2 + c] - dot(l10, v0)
        qcat[c] = rhs3(jnp.concatenate([dot(ginv_ref[c, 0], v0), dot(ginv_ref[c, 1], v1)], axis=0))
    loads[1].wait()

    def slab(dz, s, dx):
        r = ring(ring(z, dz), -y)
        slot = slot_of(r, s)
        c = (slot >= 3).astype(jnp.int32)
        t = jnp.maximum(slot - 3 * c, 0)
        m = lax.rem(x + dx - pick(offs, slot) // 4 - (y + r) // 4 + 8, 4)
        w0 = w1[0, c, m, t].reshape(B, B)
        wb = w1[0, 2 + c, m, t].reshape(B, B) - mul3(lhs3(w0), lt[c])
        full = jnp.concatenate([w0, wb], axis=1)
        return fr[c, 4 * t + m] - mul3(lhs3(full), qcat[c])

    def z_device(dz):
        return (f, y, 4 * x + ring(z, dz))

    def x_device(dx):
        return (f, y, 4 * ring(x, dx) + z)

    def first(s, dz, dx):
        sem = (h1s.at[s, dz, dx], h1r.at[s, dz, dx])
        src = stg.at[s, dz, dx]
        if dz and (s == 0 or not dx):
            dst = hop.at[s, dz, dx] if dx else fin.at[s, dx, dz]
            return remote(src, dst, *sem, z_device(dz))
        dst = hop.at[s, dz, dx] if dz else fin.at[s, dx, dz]
        return remote(src, dst, *sem, x_device(dx))

    def second(s, dz, dx):
        sem = (h2s.at[s, dz, dx], h2r.at[s, dz, dx])
        device = x_device(dx) if s == 0 else z_device(dz)
        return remote(hop.at[s, dz, dx], fin.at[s, dx, dz], *sem, device)

    def begin(s, dz, dx):
        if not (dz or dx):
            fin[s, 0, 0] = slab(0, s, 0)
            return
        stg[s, dz, dx] = slab(dz, s, dx)
        first(s, dz, dx).start()

    order = [(0, 0, 0)] + [(0, dz, 0) for dz in AROUND]
    for d in AROUND:
        order += [(1, d, dx) for dx in AROUND]
        order += [(0, dz, d) for dz in AROUND]
    order += [(1, 0, 0)]
    for d in AROUND:
        order += [(1, 0, d), (0, 0, d), (1, d, 0)]
    for item in order:
        begin(*item)

    def pass_y(s, dx):
        for dz in range(4):
            if dz and dx:
                second(s, dz, dx).wait_recv()
            elif dz or dx:
                first(s, dz, dx).wait_recv()
        slot = slot_of(ring(z, -y), s)
        for dy in (1, 3, 2, 0):
            for t in range(3):
                res = jnp.where(slot >= 3, residues[3 + t], residues[t])
                dz = lax.rem(z - ring(y, dy) + res + 8, 4)
                block = pick([fin[s, dx, k, :, t * B : (t + 1) * B] for k in range(4)], dz)
                if dy:
                    sy[dy, s, dx, t] = block
                else:
                    got[0, s, dx, t] = block
            if dy:
                y_copy(dy, s, dx).start()

    def y_copy(dy, s, dx):
        return remote(
            sy.at[dy, s, dx], got.at[dy, s, dx], ys.at[dy, s, dx], yr.at[dy, s, dx], (f, ring(y, dy), 4 * x + z)
        )

    def forward(s, d):
        for e in AROUND:
            dz, dx = (e, d) if s == 0 else (d, e)
            first(s, dz, dx).wait_recv()
            second(s, dz, dx).start()

    forward(1, 1)
    pass_y(0, 0)
    forward(0, 1)
    forward(1, 3)
    forward(0, 3)
    forward(1, 2)
    forward(0, 2)
    pass_y(1, 0)
    for dx in AROUND:
        pass_y(0, dx)
        pass_y(1, dx)
    for s in range(2):
        for dx in range(4):
            for dy in AROUND:
                y_copy(dy, s, dx).wait_recv()

    loads[2].wait()

    def landing(c, target):
        block, found = jnp.int32(0), jnp.bool_(False)
        for t in range(3):
            j = 16 * t + lax.rem(target - offs[3 * c + t] + 96 * 16, 16)
            hit = map_ref[c, j] == target
            block = jnp.where(hit, j, block)
            found = found | hit
        return block, found

    col_hits = [[landing(c, 32 * v + 16 * f + 4 * x + z) for v in range(3)] for c in range(2)]

    def add_row(u):
        for c in range(2):
            j, row_found = landing(c, 4 * u + y)
            dx = lax.rem(x - lax.rem(j, 16) // 4 + 4, 4)
            t_j = j // 16
            for v in range(3):
                i, col_found = col_hits[c][v]
                dy = lax.rem(y - lax.rem(i, 4) + 4, 4)
                s = jnp.minimum(pick(ranks[3 * c : 3 * c + 3], i // 16), 1)
                block = got[dy, s, dx, t_j]
                lanes = slice(v * B, (v + 1) * B)
                acc[u, :, lanes] += jnp.where(row_found & col_found, block, 0.0).T

    def add_rows(low, high):
        def step(u, _):
            add_row(u)
            return 0

        lax.fori_loop(low, high, step, 0)

    add_rows(0, 2)
    for i in range(2):
        for t in range(3):
            loct[2 + i, t] = turned(acc[i, :, t * B : (t + 1) * B])

    bounds = [(2, 5), (5, 8), (8, 24)]
    finish2 = gather(
        PARENT_PANELS, True, PARENT_COUPLINGS, acc, loct.at[2:4], u2, w2, pp2, sems[12:24],
        lambda n: add_rows(*bounds[n]),
    )
    store = pltpu.make_async_copy(acc, a_ref, load_sem.at[0])
    store.start()
    finish1()
    finish2()
    for s in range(2):
        for dz in range(4):
            for dx in range(4):
                if dz or dx:
                    first(s, dz, dx).wait_send()
                if dz and dx:
                    second(s, dz, dx).wait_send()
        for dx in range(4):
            for dy in AROUND:
                y_copy(dy, s, dx).wait_send()
    store.wait()


def assemble(block_map, children, parent, inverses):
    slab = (B, 3 * B)
    return pl.pallas_call(
        assemble_kernel,
        out_shape=(
            jax.ShapeDtypeStruct((24,) + slab, F32),
            jax.ShapeDtypeStruct((5,) + slab, F32),
            jax.ShapeDtypeStruct((2, 5, 4, 3) + TILE, F32),
            jax.ShapeDtypeStruct((10,) + TILE, F32),
        ),
        in_specs=[SMEM, ANY, ANY, VMEM],
        out_specs=(ANY, ANY, ANY, ANY),
        scratch_shapes=[
            pltpu.VMEM((2, 12) + slab, F32),
            pltpu.VMEM((24,) + slab, F32),
            pltpu.VMEM((4, 3) + TILE, F32),
            pltpu.VMEM((4,) + slab, F32),
            pltpu.VMEM((1, 4, 4, 3) + TILE, F32),
            pltpu.VMEM((2,) + TILE, F32),
            pltpu.VMEM((2, 3 * B, B), BF16),
            pltpu.VMEM((2, 6 * B, 3 * B), BF16),
            pltpu.VMEM((2, 4, 4) + slab, F32),
            pltpu.VMEM((2, 4, 4) + slab, F32),
            pltpu.VMEM((2, 4, 4) + slab, F32),
            pltpu.VMEM((4, 2, 4, 3, B, B), F32),
            pltpu.VMEM((4, 2, 4, 3, B, B), F32),
            DMA((3,)),
            DMA((2, 4, 4)),
            DMA((2, 4, 4)),
            DMA((2, 4, 4)),
            DMA((2, 4, 4)),
            DMA((4, 2, 4)),
            DMA((4, 2, 4)),
        ]
        + gather_sems(4, 1)
        + gather_sems(5, 4),
        compiler_params=pltpu.CompilerParams(
            collective_id=0, has_side_effects=True, vmem_limit_bytes=58 << 20
        ),
        name="assemble",
    )(block_map, children.reshape((2, 12) + slab), parent.reshape((24,) + slab), inverses)


def parent_kernel(a_ref, u_ref, w_ref, pp_ref, g_ref, out_ref, cur, ltc, v_ref, q_ref, qcat, gcat, wt):
    f, y, x, z = place()
    steps = range(5)
    col = 4 * x + z
    n = pl.program_id(0)

    @pl.when(n == 0)
    def _():
        for k in range(10):
            cur[k] = pp_ref[k].reshape(B, B)
        for j in steps:
            v_ref[j] = u_ref[j]
        for j in range(4):
            for k in range(j + 1, 5):
                l_kj = dot(cur[PAIR[k, j]], g_ref[j])
                ltc[PAIR[k, j]] = l_kj.T
                for i in range(j + 1, k):
                    cur[PAIR[k, i]] -= dot(l_kj, cur[PAIR[i, j]].T)
                v_ref[k] -= dot(l_kj, v_ref[j])
        for k in steps:
            q_ref[k * B : (k + 1) * B, :] = dot(g_ref[k], v_ref[k])
            gcat[k] = rhs3(g_ref[k])
        qcat[...] = rhs3(q_ref[...])

    for k in steps:
        w = w_ref[0, k, :, 0].reshape(4 * B, B)
        if k:
            low = jnp.concatenate([ltc[PAIR[k, j]] for j in range(k)], axis=0)
            w = w - dot(wt[:, 0 : k * B], low)
        wt[:, k * B : (k + 1) * B] = w
    out = a_ref[...].reshape(4 * B, 3 * B) - mul3(lhs3(wt[...]), qcat[...])
    out_ref[...] = out.reshape(4, B, 3 * B)

    @pl.when((f == 0) & (col < 5))
    def _():
        for k in steps:

            @pl.when(col == k)
            def _():
                scaled = mul3(lhs3(wt[:, k * B : (k + 1) * B]), gcat[k])
                for i in range(4):
                    slot = 4 * n + i
                    row = 4 * slot + y

                    @pl.when(row > k)
                    def _():
                        out_ref[i, :, 0:B] = scaled[i * B : (i + 1) * B, :]

                    @pl.when(row == k)
                    def _():
                        out_ref[i, :, 0:B] = v_ref[k, :, 0:B]

    @pl.when(n == 0)
    def _():
        for k in steps:

            @pl.when(y == k % 4)
            def _():
                panel = q_ref[k * B : (k + 1) * B, :]
                keep = (f == 0) & (col <= k)
                out_ref[k // 4, :, B:] = panel[:, B:]
                out_ref[k // 4, :, 0:B] = jnp.where(keep, out_ref[k // 4, :, 0:B], panel[:, 0:B])


def parent_update(a, u, w, pp, inverses):
    def whole(shape):
        return pl.BlockSpec(shape, lambda n: (0,) * len(shape))

    return pl.pallas_call(
        parent_kernel,
        out_shape=jax.ShapeDtypeStruct((24, B, 3 * B), F32),
        grid=(6,),
        in_specs=[
            pl.BlockSpec((4, B, 3 * B), lambda n: (n, 0, 0)),
            whole((5, B, 3 * B)),
            pl.BlockSpec((1, 5, 4, 1) + TILE, lambda n: (n % 2, 0, 0, n // 2, 0, 0, 0, 0)),
            whole((10,) + TILE),
            whole((5, B, B)),
        ],
        out_specs=pl.BlockSpec((4, B, 3 * B), lambda n: (n, 0, 0)),
        scratch_shapes=[
            pltpu.VMEM((10, B, B), F32),
            pltpu.VMEM((10, B, B), F32),
            pltpu.VMEM((5, B, 3 * B), F32),
            pltpu.VMEM((5 * B, 3 * B), F32),
            pltpu.VMEM((15 * B, 3 * B), BF16),
            pltpu.VMEM((5, 3 * B, B), BF16),
            pltpu.VMEM((4 * B, 5 * B), F32),
        ],
        compiler_params=pltpu.CompilerParams(vmem_limit_bytes=48 << 20),
        name="parent_update",
    )(a, u, w, pp, inverses)


def body(child_fronts, parent_front, child_inverses, parent_inverses, block_map):
    a, u, w, pp = assemble(block_map, child_fronts, parent_front, child_inverses)
    return parent_update(a, u, w, pp, parent_inverses).reshape(parent_front.shape)


def solution(mesh):
    placed = (
        P("front", "row", "col"),
        P("row", ("front", "col")),
        P("front", None, None, None),
        P(),
        P("front", None),
    )
    return jax.shard_map(
        body, mesh=mesh, in_specs=placed, out_specs=P("row", ("front", "col")), check_vma=False
    )
```

```python
import functools

import jax
import jax.numpy as jnp
from jax import lax
from jax.experimental import pallas as pl
from jax.experimental.pallas import tpu as pltpu
from jax.sharding import PartitionSpec as P

MESH = pl.DeviceIdType.MESH
F32, BF16 = jnp.float32, jnp.bfloat16
ANY = pl.BlockSpec(memory_space=pltpu.HBM)
VMEM = pl.BlockSpec(memory_space=pltpu.VMEM)
SMEM = pl.BlockSpec(memory_space=pltpu.SMEM)
DMA = pltpu.SemaphoreType.DMA
B = 128
AROUND = (1, 3, 2)
HALF = 64
TILE = (4, 2, 16, B)


def split(a):
    high = a.astype(BF16)
    return high, (a - high.astype(F32)).astype(BF16)


def lhs3(a):
    high, low = split(a)
    return jnp.concatenate([high, high, low], axis=1)


def rhs3(b):
    high, low = split(b)
    return jnp.concatenate([high, low, high], axis=0)


def mul3(a, b):
    return jnp.dot(a, b, preferred_element_type=F32)


def dot(a, b):
    return mul3(lhs3(a), rhs3(b))


def place():
    col = lax.axis_index("col")
    return lax.axis_index("front"), lax.axis_index("row"), col // 4, col % 4


def ring(i, d):
    return lax.rem(i + d + 4, 4)


def remote(src, dst, ssem, rsem, device):
    return pltpu.make_async_remote_copy(
        src_ref=src, dst_ref=dst, send_sem=ssem, recv_sem=rsem, device_id=device, device_id_type=MESH
    )


def pick(values, index):
    out = values[0]
    for i in range(1, len(values)):
        out = jnp.where(index == i, values[i], out)
    return out


def gather(panels, cross, couplings, loc, loct, u_ref, w_ref, pp_ref, sems, idle):
    su, ru, ss, rs, s2, r2, s3, r3, s4, r4, s5, r5 = sems
    f, y, x, z = place()
    own = f if cross else 0
    parts = (slice(0, 1), slice(1, 3)) if cross else (slice(0, 3),)
    late = []

    def scatter(p, op):
        i = panels[p][1]
        for zz in range(4):
            mine = (y == z) & (z == zz)
            src, dst = loct.at[i, :, zz], w_ref.at[own, p, x, :, zz]
            cp = remote(src, dst, ss.at[p, zz], rs.at[p], (f, z, 4 * x + zz))
            here = pltpu.make_async_copy(src, dst, ss.at[p, zz])

            @pl.when(jnp.logical_not(mine))
            def _():
                cp.start() if op == "start" else cp.wait_send()

            @pl.when(mine)
            def _():
                here.start() if op == "start" else here.wait()

    def column(p, op):
        i = panels[p][1]
        for dy in AROUND:
            cp = remote(loc.at[i], u_ref.at[p], su.at[p, dy], ru.at[p], (f, ring(y, dy), 4 * x + z))
            cp.start() if op == "start" else cp.wait_send()
        here = pltpu.make_async_copy(loc.at[i], u_ref.at[p], su.at[p, 0])
        here.start() if op == "start" else here.wait()

    for p, (sy, i) in enumerate(panels):
        pl.when(y == sy)(functools.partial(scatter, p, "start"))
    idle(0)
    for p, (sy, i) in enumerate(panels):
        region = w_ref.at[own, p, x, :, z]

        @pl.when(jnp.logical_not((y == sy) & (y == z)))
        def _():
            remote(region, region, ss.at[p, 0], rs.at[p], (f, y, 4 * x + z)).wait_recv()

        @pl.when((y == sy) & (y == z))
        def _():
            for zz in range(4):

                @pl.when(z == zz)
                def _():
                    pltpu.make_async_copy(region, region, ss.at[p, zz]).wait()

    along_x = [w_ref.at[own, :, ring(x, -d), :, z, 0] for d in range(4)]
    along_z = [w_ref.at[own, :, x, :, ring(z, -d), 1] for d in range(4)]

    def part_x(d, ts, front=own):
        return w_ref.at[front, :, :, ts, ring(z, -d), 0]

    def part_z(d, ts, front=own):
        return w_ref.at[front, :, ring(x, -d), ts, :, 1]

    def send(*args):
        cp = remote(*args)
        cp.start()
        late.append(cp)

    def arrived(region, rsem):
        remote(region, region, s2.at[0, 0], rsem, (f, y, 4 * x + z)).wait_recv()

    def across(q, n, region):
        if cross:
            send(region, region, s4.at[q, n], r4.at[q, n], (1 - f, y, 4 * x + z))

    for d in AROUND:
        send(along_x[0], along_x[0], s2.at[0, d], r2.at[0, d], (f, y, 4 * ring(x, d) + z))
        send(along_z[0], along_z[0], s2.at[1, d], r2.at[1, d], (f, y, 4 * x + ring(z, d)))
    for p, (sy, i) in enumerate(panels):
        pl.when(y == sy)(functools.partial(column, p, "start"))
    idle(1)
    for d in AROUND:
        arrived(along_x[d], r2.at[0, d])
    for q, ts in enumerate(parts):
        for d in AROUND:
            region = part_x(0, ts)
            send(region, region, s3.at[0, q, d], r3.at[0, q, d], (f, y, 4 * x + ring(z, d)))
    for d in AROUND:
        arrived(along_z[d], r2.at[1, d])
    for q, ts in enumerate(parts):
        for d in AROUND:
            region = part_z(0, ts)
            send(region, region, s3.at[1, q, d], r3.at[1, q, d], (f, y, 4 * ring(x, d) + z))
    for q, ts in enumerate(parts):
        across(q, 0, part_x(0, ts))
        across(q, 4, part_z(0, ts))
    idle(2)

    def collect(q, ts):
        for d in AROUND:
            arrived(part_x(d, ts), r3.at[0, q, d])
            across(q, d, part_x(d, ts))
            arrived(part_z(d, ts), r3.at[1, q, d])
            across(q, 4 + d, part_z(d, ts))

    collect(0, parts[0])
    if cross:

        def couple(e, op):
            sy, base, n, m = couplings[e]
            src, dst = w_ref.at[0, 0:n, m, 0], pp_ref.at[base : base + n]
            for dy in AROUND:
                cp = remote(src, dst, s5.at[e, dy], r5.at[e], (f, ring(y, dy), 4 * x + z))
                cp.start() if op == "start" else cp.wait_send()
            here = pltpu.make_async_copy(src, dst, s5.at[e, 0])
            here.start() if op == "start" else here.wait()

        pair = remote(pp_ref, pp_ref, s4.at[0, 8], r4.at[0, 8], (1 - f, y, 4 * x + z))

        @pl.when(f == 0)
        def _():
            for e, (sy, base, n, m) in enumerate(couplings):
                pl.when(y == sy)(functools.partial(couple, e, "start"))

    for q in range(1, len(parts)):
        collect(q, parts[q])
    if cross:

        @pl.when(f == 0)
        def _():
            for e, (sy, base, n, m) in enumerate(couplings):

                @pl.when(y != sy)
                def _():
                    arrived(pp_ref.at[base : base + n], r5.at[e])

                pl.when(y == sy)(functools.partial(couple, e, "wait"))
            pair.start()

    for p, (sy, i) in enumerate(panels):

        @pl.when(y != sy)
        def _():
            arrived(u_ref.at[p], ru.at[p])

    if cross:
        for q, ts in enumerate(parts):
            for d in range(4):
                arrived(part_x(d, ts, 1 - f), r4.at[q, d])
                arrived(part_z(d, ts, 1 - f), r4.at[q, 4 + d])

        @pl.when(f == 0)
        def _():
            pair.wait_send()

        @pl.when(f == 1)
        def _():
            pair.wait_recv()

    def finish():
        def scatter_rest(p):
            i = panels[p][1]
            for zz in range(4):

                @pl.when(jnp.logical_not((y == z) & (z == zz)))
                def _():
                    src, dst = loct.at[i, :, zz], w_ref.at[own, p, x, :, zz]
                    remote(src, dst, ss.at[p, zz], rs.at[p], (f, z, 4 * x + zz)).wait_send()

        for p, (sy, i) in enumerate(panels):
            pl.when(y == sy)(functools.partial(scatter_rest, p))
        for cp in late:
            cp.wait_send()

    for p, (sy, i) in enumerate(panels):
        pl.when(y == sy)(functools.partial(column, p, "wait"))
    return finish


def gather_sems(count, couplings):
    return [
        DMA((count, 4)),
        DMA((count,)),
        DMA((count, 4)),
        DMA((count,)),
        DMA((2, 4)),
        DMA((2, 4)),
        DMA((2, 2, 4)),
        DMA((2, 2, 4)),
        DMA((2, 9)),
        DMA((2, 9)),
        DMA((couplings, 4)),
        DMA((couplings,)),
    ]


CHILD_PANELS = ((0, 0), (0, 1), (1, 0), (1, 1))
PARENT_PANELS = ((0, 0), (1, 0), (2, 0), (3, 0), (0, 1))
PARENT_COUPLINGS = ((1, 0, 1, 0), (2, 1, 2, 0), (3, 3, 3, 0), (0, 6, 4, 1))
PAIR = {(1, 0): 0, (2, 0): 1, (2, 1): 2, (3, 0): 3, (3, 1): 4, (3, 2): 5, (4, 0): 6, (4, 1): 7, (4, 2): 8, (4, 3): 9}


def assemble_kernel(
    map_ref, child_ref, parent_ref, ginv_ref, a_ref, u2, w2, pp2,
    fr, acc, loct, u1, w1, pp1, lt, qcat, stg, hop, fin, sy, got, load_sem, tree_s, tree_r, h1s, h1r, h2s, h2r, ys, yr, *sems
):
    f, y, x, z = place()
    here = (f, y, 4 * x + z)

    loads = [
        pltpu.make_async_copy(child_ref.at[:, 0:1], fr.at[:, 0:1], load_sem.at[0]),
        pltpu.make_async_copy(child_ref.at[:, 1:12], fr.at[:, 1:12], load_sem.at[1]),
        pltpu.make_async_copy(parent_ref, acc, load_sem.at[2]),
    ]
    for cp in loads:
        cp.start()

    barrier = pltpu.get_barrier_semaphore()
    greeted = []
    for dy in range(4):
        for dz in range(4):
            if dy or dz:
                greeted.append((f, ring(y, dy), 4 * x + ring(z, dz)))
    for dx in range(1, 4):
        greeted.append((f, y, 4 * ring(x, dx) + z))
    greeted.append((1 - f, y, 4 * x + z))
    for device in greeted:
        pl.semaphore_signal(barrier, inc=1, device_id=device, device_id_type=MESH)

    def turned(block):
        return block.T.reshape(TILE)

    offs = [lax.rem(map_ref[c, 16 * t + 3] - 3 + 16, 16) for c in range(2) for t in range(3)]
    residues = [lax.rem(o, 4) for o in offs]
    ranks = []
    for i in range(6):
        rank = jnp.int32(0)
        for k in range(i):
            rank = rank + (residues[k] == residues[i]).astype(jnp.int32)
        ranks.append(rank)

    def slot_of(r, s):
        slot = jnp.int32(-1)
        for i in range(6):
            slot = jnp.where((residues[i] == r) & (ranks[i] == s), i, slot)
        return slot

    loads[0].wait()
    for c in range(2):
        for t in range(3):
            loct[c, t] = turned(fr[c, 0, :, t * B : (t + 1) * B])
    pl.semaphore_wait(barrier, len(greeted))

    first_rows = fr.at[:, 0]

    def tree_y(op):
        src = fr.at[:, 0, :, 0:B]
        for dy in AROUND:
            cp = remote(src, pp1, tree_s.at[0, dy], tree_r.at[0], (f, ring(y, dy), 4 * x + z))
            cp.start() if op == "start" else cp.wait_send()
        cp = pltpu.make_async_copy(src, pp1, tree_s.at[0, 0])
        cp.start() if op == "start" else cp.wait()

    def tree(axis, op):
        for d in AROUND:
            device = (f, y, 4 * ring(x, d) + z) if axis == 1 else (f, y, 4 * x + ring(z, d))
            cp = remote(pp1, pp1, tree_s.at[axis, d], tree_r.at[axis], device)
            cp.start() if op == "start" else cp.wait_send()

    def tree_wait(axis):
        remote(pp1, pp1, tree_s.at[axis, 0], tree_r.at[axis], here).wait_recv()

    root, line, floor = (y == 1) & (x == 0) & (z == 0), (x == 0) & (z == 0), z == 0

    def couple_child(n):
        if n == 0:

            @pl.when(root)
            def _():
                tree_y("start")

        if n == 1:

            @pl.when(root)
            def _():
                tree_y("wait")

            @pl.when(line & jnp.logical_not(root))
            def _():
                tree_wait(0)

            @pl.when(line)
            def _():
                tree(1, "start")

        if n == 2:

            @pl.when(floor & jnp.logical_not(line))
            def _():
                tree_wait(1)

            @pl.when(floor)
            def _():
                tree(2, "start")

    finish1 = gather(CHILD_PANELS, False, (), first_rows, loct, u1, w1, None, sems[0:12], couple_child)

    @pl.when(jnp.logical_not(floor))
    def _():
        tree_wait(2)

    @pl.when(line)
    def _():
        tree(1, "wait")

    @pl.when(floor)
    def _():
        tree(2, "wait")

    for c in range(2):
        l10 = dot(pp1[c], ginv_ref[c, 0])
        lt[c] = rhs3(l10.T)
        v0 = u1[c]
        v1 = u1[2 + c] - dot(l10, v0)
        qcat[c] = rhs3(jnp.concatenate([dot(ginv_ref[c, 0], v0), dot(ginv_ref[c, 1], v1)], axis=0))
    loads[1].wait()

    def slab(dz, s, dx):
        r = ring(ring(z, dz), -y)
        slot = slot_of(r, s)
        c = (slot >= 3).astype(jnp.int32)
        t = jnp.maximum(slot - 3 * c, 0)
        m = lax.rem(x + dx - pick(offs, slot) // 4 - (y + r) // 4 + 8, 4)
        w0 = w1[0, c, m, t].reshape(B, B)
        wb = w1[0, 2 + c, m, t].reshape(B, B) - mul3(lhs3(w0), lt[c])
        full = jnp.concatenate([w0, wb], axis=1)
        return fr[c, 4 * t + m] - mul3(lhs3(full), qcat[c])

    def z_device(dz):
        return (f, y, 4 * x + ring(z, dz))

    def x_device(dx):
        return (f, y, 4 * ring(x, dx) + z)

    def first(s, h, dz, dx):
        sem = (h1s.at[s, h, dz, dx], h1r.at[s, h, dz, dx])
        rows = pl.ds(h * HALF, HALF)
        src = stg.at[s, dz, dx, rows]
        if not dx:
            return remote(src, fin.at[s, dx, dz, rows], *sem, z_device(dz))
        dst = hop.at[s, dz, dx, rows] if dz else fin.at[s, dx, dz, rows]
        return remote(src, dst, *sem, x_device(dx))

    def second(s, h, dz, dx):
        sem = (h2s.at[s, h, dz, dx], h2r.at[s, h, dz, dx])
        rows = pl.ds(h * HALF, HALF)
        return remote(hop.at[s, dz, dx, rows], fin.at[s, dx, dz, rows], *sem, z_device(dz))

    def compute(s, items):
        for dz, dx in items:
            if dz or dx:
                stg[s, dz, dx] = slab(dz, s, dx)
            else:
                fin[s, 0, 0] = slab(0, s, 0)

    def start(s, h, items):
        for dz, dx in items:
            first(s, h, dz, dx).start()

    own = [(0, 0)]
    straight = [(dz, 0) for dz in AROUND]
    rounds = [[(dz, dx) for dx in AROUND] for dz in (1, 3, 2, 0)]

    def forward(s, h, dx):
        for dz in AROUND:
            first(s, h, dz, dx).wait_recv()
            second(s, h, dz, dx).start()

    def y_copy(dy, s, h, dx):
        rows = pl.ds(h * HALF, HALF)
        sem = (ys.at[dy, s, h, dx], yr.at[dy, s, h, dx])
        return remote(sy.at[dy, s, dx, :, rows], got.at[dy, s, dx, :, rows], *sem, (f, ring(y, dy), 4 * x + z))

    home = ring(z, -y)
    child_of = [(slot_of(home, s) >= 3) for s in range(2)]

    def pass_y(s, h, dx):
        for dz in range(4):
            if dz and dx:
                second(s, h, dz, dx).wait_recv()
            elif dz or dx:
                first(s, h, dz, dx).wait_recv()
        rows = slice(h * HALF, (h + 1) * HALF)
        for dy in (1, 3, 2, 0):
            for t in range(3):
                res = jnp.where(child_of[s], residues[3 + t], residues[t])
                dz = lax.rem(z - ring(y, dy) + res + 8, 4)
                block = pick([fin[s, dx, k, rows, t * B : (t + 1) * B] for k in range(4)], dz)
                if dy:
                    sy[dy, s, dx, t, rows, :] = block
                else:
                    got[0, s, dx, t, rows, :] = block
            if dy:
                y_copy(dy, s, h, dx).start()

    compute(0, straight)
    start(0, 0, straight)
    for items in rounds:
        compute(0, items)
        start(0, 0, items)
    compute(0, own)
    start(0, 1, straight)
    for items in rounds:
        start(0, 1, items)
    pass_y(0, 0, 0)
    compute(1, straight + own)
    start(1, 0, straight)
    pass_y(0, 1, 0)
    forward(0, 0, 1)
    compute(1, rounds[0])
    start(1, 0, rounds[0])
    forward(0, 0, 3)
    compute(1, rounds[1])
    start(1, 0, rounds[1])
    pass_y(0, 0, 1)
    forward(0, 0, 2)
    compute(1, rounds[2])
    start(1, 0, rounds[2])
    pass_y(0, 0, 3)
    compute(1, rounds[3])
    start(1, 0, rounds[3])
    start(1, 1, straight)
    for items in rounds:
        start(1, 1, items)
    pass_y(1, 0, 0)
    pass_y(0, 0, 2)
    forward(0, 1, 1)
    forward(0, 1, 3)
    pass_y(0, 1, 1)
    forward(0, 1, 2)
    pass_y(0, 1, 3)
    pass_y(1, 1, 0)
    pass_y(0, 1, 2)
    for h in range(2):
        forward(1, h, 1)
        forward(1, h, 3)
        pass_y(1, h, 1)
        forward(1, h, 2)
        pass_y(1, h, 3)
        pass_y(1, h, 2)
    halves = [(s, h) for s in range(2) for h in range(2)]
    for s, h in halves:
        for dx in range(4):
            for dy in AROUND:
                y_copy(dy, s, h, dx).wait_recv()

    loads[2].wait()

    def landing(c, target):
        block, found = jnp.int32(0), jnp.bool_(False)
        for t in range(3):
            j = 16 * t + lax.rem(target - offs[3 * c + t] + 96 * 16, 16)
            hit = map_ref[c, j] == target
            block = jnp.where(hit, j, block)
            found = found | hit
        return block, found

    col_hits = [[landing(c, 32 * v + 16 * f + 4 * x + z) for v in range(3)] for c in range(2)]

    def add_row(u):
        for c in range(2):
            j, row_found = landing(c, 4 * u + y)
            dx = lax.rem(x - lax.rem(j, 16) // 4 + 4, 4)
            t_j = j // 16
            for v in range(3):
                i, col_found = col_hits[c][v]
                dy = lax.rem(y - lax.rem(i, 4) + 4, 4)
                s = jnp.minimum(pick(ranks[3 * c : 3 * c + 3], i // 16), 1)
                block = got[dy, s, dx, t_j]
                lanes = slice(v * B, (v + 1) * B)
                acc[u, :, lanes] += jnp.where(row_found & col_found, block, 0.0).T

    def add_rows(low, high):
        def step(u, _):
            add_row(u)
            return 0

        lax.fori_loop(low, high, step, 0)

    add_rows(0, 2)
    for i in range(2):
        for t in range(3):
            loct[2 + i, t] = turned(acc[i, :, t * B : (t + 1) * B])

    store = pltpu.make_async_copy(acc, a_ref, load_sem.at[0])
    bounds = [(2, 5), (5, 8), (8, 24)]

    def add_rest(n):
        add_rows(*bounds[n])
        if n == 2:
            store.start()

    finish2 = gather(
        PARENT_PANELS, True, PARENT_COUPLINGS, acc, loct.at[2:4], u2, w2, pp2, sems[12:24],
        add_rest,
    )
    finish1()
    finish2()
    for s, h in halves:
        for dz in range(4):
            for dx in range(4):
                if dz or dx:
                    first(s, h, dz, dx).wait_send()
                if dz and dx:
                    second(s, h, dz, dx).wait_send()
        for dx in range(4):
            for dy in AROUND:
                y_copy(dy, s, h, dx).wait_send()
    store.wait()


def assemble(block_map, children, parent, inverses):
    slab = (B, 3 * B)
    return pl.pallas_call(
        assemble_kernel,
        out_shape=(
            jax.ShapeDtypeStruct((24,) + slab, F32),
            jax.ShapeDtypeStruct((5,) + slab, F32),
            jax.ShapeDtypeStruct((2, 5, 4, 3) + TILE, F32),
            jax.ShapeDtypeStruct((10,) + TILE, F32),
        ),
        in_specs=[SMEM, ANY, ANY, VMEM],
        out_specs=(ANY, ANY, ANY, ANY),
        scratch_shapes=[
            pltpu.VMEM((2, 12) + slab, F32),
            pltpu.VMEM((24,) + slab, F32),
            pltpu.VMEM((4, 3) + TILE, F32),
            pltpu.VMEM((4,) + slab, F32),
            pltpu.VMEM((1, 4, 4, 3) + TILE, F32),
            pltpu.VMEM((2, B, B), F32),
            pltpu.VMEM((2, 3 * B, B), BF16),
            pltpu.VMEM((2, 6 * B, 3 * B), BF16),
            pltpu.VMEM((2, 4, 4) + slab, F32),
            pltpu.VMEM((2, 4, 4) + slab, F32),
            pltpu.VMEM((2, 4, 4) + slab, F32),
            pltpu.VMEM((4, 2, 4, 3, B, B), F32),
            pltpu.VMEM((4, 2, 4, 3, B, B), F32),
            DMA((3,)),
            DMA((3, 4)),
            DMA((3,)),
            DMA((2, 2, 4, 4)),
            DMA((2, 2, 4, 4)),
            DMA((2, 2, 4, 4)),
            DMA((2, 2, 4, 4)),
            DMA((4, 2, 2, 4)),
            DMA((4, 2, 2, 4)),
        ]
        + gather_sems(4, 1)
        + gather_sems(5, 4),
        compiler_params=pltpu.CompilerParams(
            collective_id=0, has_side_effects=True, vmem_limit_bytes=58 << 20
        ),
        name="assemble",
    )(block_map, children.reshape((2, 12) + slab), parent.reshape((24,) + slab), inverses)


def parent_kernel(a_ref, u_ref, w_ref, pp_ref, g_ref, out_ref, panel, lth, ltl, q_ref, qcat, gcat, wh, wl):
    f, y, x, z = place()
    steps = range(5)
    col = 4 * x + z
    n = pl.program_id(0)

    @pl.when(n == 0)
    def _():
        for k in steps:
            for j in range(k):
                block = pp_ref[PAIR[k, j]].reshape(B, B)
                panel[k * B : (k + 1) * B, j * B : (j + 1) * B] = block
                panel[j * B : (j + 1) * B, k * B : (k + 1) * B] = block.T
            panel[k * B : (k + 1) * B, k * B : (k + 1) * B] = jnp.zeros((B, B), F32)
            panel[k * B : (k + 1) * B, 5 * B :] = u_ref[k]
            gcat[k] = rhs3(g_ref[k])
        for j in range(4):
            here, later = slice(j * B, (j + 1) * B), slice((j + 1) * B, 5 * B)
            low = mul3(lhs3(panel[later, here]), gcat[j])
            high, rest = split(low.T)
            lth[here, later] = high
            ltl[here, later] = rest
            panel[later, (j + 1) * B :] -= dot(low, panel[here, (j + 1) * B :])
        for k in steps:
            q_ref[k * B : (k + 1) * B, :] = dot(g_ref[k], panel[k * B : (k + 1) * B, 5 * B :])
        qcat[...] = rhs3(q_ref[...])

    def keep(k, w):
        high, rest = split(w)
        wh[:, k * B : (k + 1) * B] = high
        wl[:, k * B : (k + 1) * B] = rest

    def left(low, high):
        return jnp.concatenate([wh[:, low:high], wh[:, low:high], wl[:, low:high]], axis=1)

    def earlier(k0, k1, j0, j1):
        rows, cols = slice(j0 * B, j1 * B), slice(k0 * B, k1 * B)
        low = jnp.concatenate([lth[rows, cols], ltl[rows, cols], lth[rows, cols]], axis=0)
        return mul3(left(j0 * B, j1 * B), low)

    raw = [w_ref[0, k, :, 0].reshape(4 * B, B) for k in steps]
    keep(0, raw[0])
    keep(1, raw[1] - earlier(1, 2, 0, 1))
    pair = jnp.concatenate([raw[2], raw[3]], axis=1) - earlier(2, 4, 0, 2)
    keep(2, pair[:, 0:B])
    keep(3, pair[:, B:] - earlier(3, 4, 2, 3))
    keep(4, raw[4] - earlier(4, 5, 0, 4))
    out = a_ref[...].reshape(4 * B, 3 * B) - mul3(left(0, 5 * B), qcat[...])
    out_ref[...] = out.reshape(4, B, 3 * B)

    @pl.when((f == 0) & (col < 5))
    def _():
        for k in steps:

            @pl.when(col == k)
            def _():
                scaled = mul3(left(k * B, (k + 1) * B), gcat[k])
                for i in range(4):
                    slot = 4 * n + i
                    row = 4 * slot + y

                    @pl.when(row > k)
                    def _():
                        out_ref[i, :, 0:B] = scaled[i * B : (i + 1) * B, :]

                    @pl.when(row == k)
                    def _():
                        out_ref[i, :, 0:B] = panel[k * B : (k + 1) * B, 5 * B : 6 * B]

    @pl.when(n == 0)
    def _():
        for k in steps:

            @pl.when(y == k % 4)
            def _():
                rows = q_ref[k * B : (k + 1) * B, :]
                done = (f == 0) & (col <= k)
                out_ref[k // 4, :, B:] = rows[:, B:]
                out_ref[k // 4, :, 0:B] = jnp.where(done, out_ref[k // 4, :, 0:B], rows[:, 0:B])


def parent_update(a, u, w, pp, inverses):
    def whole(shape):
        return pl.BlockSpec(shape, lambda n: (0,) * len(shape))

    return pl.pallas_call(
        parent_kernel,
        out_shape=jax.ShapeDtypeStruct((24, B, 3 * B), F32),
        grid=(6,),
        in_specs=[
            pl.BlockSpec((4, B, 3 * B), lambda n: (n, 0, 0)),
            whole((5, B, 3 * B)),
            pl.BlockSpec((1, 5, 4, 1) + TILE, lambda n: (n % 2, 0, 0, n // 2, 0, 0, 0, 0)),
            whole((10,) + TILE),
            whole((5, B, B)),
        ],
        out_specs=pl.BlockSpec((4, B, 3 * B), lambda n: (n, 0, 0)),
        scratch_shapes=[
            pltpu.VMEM((5 * B, 8 * B), F32),
            pltpu.VMEM((5 * B, 5 * B), BF16),
            pltpu.VMEM((5 * B, 5 * B), BF16),
            pltpu.VMEM((5 * B, 3 * B), F32),
            pltpu.VMEM((15 * B, 3 * B), BF16),
            pltpu.VMEM((5, 3 * B, B), BF16),
            pltpu.VMEM((4 * B, 5 * B), BF16),
            pltpu.VMEM((4 * B, 5 * B), BF16),
        ],
        compiler_params=pltpu.CompilerParams(vmem_limit_bytes=48 << 20),
        name="parent_update",
    )(a, u, w, pp, inverses)


def body(child_fronts, parent_front, child_inverses, parent_inverses, block_map):
    a, u, w, pp = assemble(block_map, child_fronts, parent_front, child_inverses)
    return parent_update(a, u, w, pp, parent_inverses).reshape(parent_front.shape)


def solution(mesh):
    placed = (
        P("front", "row", "col"),
        P("row", ("front", "col")),
        P("front", None, None, None),
        P(),
        P("front", None),
    )
    return jax.shard_map(
        body, mesh=mesh, in_specs=placed, out_specs=P("row", ("front", "col")), check_vma=False
    )
```

```python
import functools

import jax
import jax.numpy as jnp
from jax import lax
from jax.experimental import pallas as pl
from jax.experimental.pallas import tpu as pltpu
from jax.sharding import PartitionSpec as P

MESH = pl.DeviceIdType.MESH
F32, BF16 = jnp.float32, jnp.bfloat16
ANY = pl.BlockSpec(memory_space=pltpu.HBM)
VMEM = pl.BlockSpec(memory_space=pltpu.VMEM)
SMEM = pl.BlockSpec(memory_space=pltpu.SMEM)
DMA = pltpu.SemaphoreType.DMA
B = 128
AROUND = (1, 3, 2)
HALF = 64
TILE = (4, 2, 16, B)


def split(a):
    high = a.astype(BF16)
    return high, (a - high.astype(F32)).astype(BF16)


def lhs3(a):
    high, low = split(a)
    return jnp.concatenate([high, high, low], axis=1)


def rhs3(b):
    high, low = split(b)
    return jnp.concatenate([high, low, high], axis=0)


def mul3(a, b):
    return jnp.dot(a, b, preferred_element_type=F32)


def dot(a, b):
    return mul3(lhs3(a), rhs3(b))


def place():
    col = lax.axis_index("col")
    return lax.axis_index("front"), lax.axis_index("row"), col // 4, col % 4


def ring(i, d):
    return lax.rem(i + d + 4, 4)


def remote(src, dst, ssem, rsem, device):
    return pltpu.make_async_remote_copy(
        src_ref=src, dst_ref=dst, send_sem=ssem, recv_sem=rsem, device_id=device, device_id_type=MESH
    )


def pick(values, index):
    out = values[0]
    for i in range(1, len(values)):
        out = jnp.where(index == i, values[i], out)
    return out


def gather(panels, own, active, cross, couplings, loc, loct, u_ref, w_ref, pp_ref, sems):
    su, ru, ss, rs, s2, r2, s3, r3, s4, r4, s5, r5 = sems
    f, y, x, z = place()
    parts = (slice(0, 1), slice(1, 3)) if cross else (slice(0, 3),)
    here, other = (f, y, 4 * x + z), (1 - f, y, 4 * x + z)
    late = []

    def stage(write):
        write() if active is None else pl.when(active)(write)

    def each(step, op):
        for p, (sy, i) in enumerate(panels):
            pl.when(y == sy)(functools.partial(step, p, op))

    def scatter(p, op):
        i = panels[p][1]
        for zz in range(4):
            mine = (y == z) & (z == zz)
            src, dst = loct(i).at[:, zz], w_ref.at[own, p, x, :, zz]
            cp = remote(src, dst, ss.at[p, zz], rs.at[p], (f, z, 4 * x + zz))

            @pl.when(jnp.logical_not(mine))
            def _():
                cp.start() if op == "start" else cp.wait_send()

            if op == "start":
                pl.when(mine)(pltpu.make_async_copy(src, dst, ss.at[p, zz]).start)

    def column(p, op):
        src = loc(panels[p][1])
        for dy in AROUND:
            cp = remote(src, u_ref.at[p], su.at[p, dy], ru.at[p], (f, ring(y, dy), 4 * x + z))
            cp.start() if op == "start" else cp.wait_send()
        local = pltpu.make_async_copy(src, u_ref.at[p], su.at[p, 0])
        local.start() if op == "start" else local.wait()

    def arrived(region, rsem):
        remote(region, region, s2.at[0, 0], rsem, here).wait_recv()

    def pieces():
        for p, (sy, i) in enumerate(panels):
            region = w_ref.at[own, p, x, :, z]

            @pl.when(jnp.logical_not((y == sy) & (y == z)))
            def _():
                arrived(region, rs.at[p])

            @pl.when((y == sy) & (y == z))
            def _():
                for zz in range(4):

                    @pl.when(z == zz)
                    def _():
                        pltpu.make_async_copy(region, region, ss.at[p, zz]).wait()

    def along_x(d):
        return w_ref.at[own, :, ring(x, -d), :, z, 0]

    def along_z(d):
        return w_ref.at[own, :, x, :, ring(z, -d), 1]

    def part_x(d, ts):
        return w_ref.at[own, :, :, ts, ring(z, -d), 0]

    def part_z(d, ts):
        return w_ref.at[own, :, ring(x, -d), ts, :, 1]

    def send(build):
        late.append(build)
        remote(*build()).start()

    def across(q, n, region):
        if cross:
            send(lambda: (region(), region(), s4.at[q, n], r4.at[q, n], other))

    def second_x():
        for d in AROUND:
            send(lambda d=d: (along_x(0), along_x(0), s2.at[0, d], r2.at[0, d], (f, y, 4 * ring(x, d) + z)))
            send(lambda d=d: (along_z(0), along_z(0), s2.at[1, d], r2.at[1, d], (f, y, 4 * x + ring(z, d))))

    def third_z():
        for d in AROUND:
            arrived(along_x(d), r2.at[0, d])
        for q, ts in enumerate(parts):
            for d in AROUND:

                def build(q=q, ts=ts, d=d):
                    region = part_x(0, ts)
                    return region, region, s3.at[0, q, d], r3.at[0, q, d], (f, y, 4 * x + ring(z, d))

                send(build)

    def third_x():
        for d in AROUND:
            arrived(along_z(d), r2.at[1, d])
        for q, ts in enumerate(parts):
            for d in AROUND:

                def build(q=q, ts=ts, d=d):
                    region = part_z(0, ts)
                    return region, region, s3.at[1, q, d], r3.at[1, q, d], (f, y, 4 * ring(x, d) + z)

                send(build)
        for q, ts in enumerate(parts):
            across(q, 0, functools.partial(part_x, 0, ts))
            across(q, 4, functools.partial(part_z, 0, ts))

    def collect(q, ts):
        for d in AROUND:
            arrived(part_x(d, ts), r3.at[0, q, d])
            across(q, d, functools.partial(part_x, d, ts))
            arrived(part_z(d, ts), r3.at[1, q, d])
            across(q, 4 + d, functools.partial(part_z, d, ts))

    def couple(e, op):
        sy, base, n, m = couplings[e]
        src, dst = w_ref.at[0, 0:n, m, 0], pp_ref.at[base : base + n]
        for dy in AROUND:
            cp = remote(src, dst, s5.at[e, dy], r5.at[e], (f, ring(y, dy), 4 * x + z))
            cp.start() if op == "start" else cp.wait_send()
        local = pltpu.make_async_copy(src, dst, s5.at[e, 0])
        local.start() if op == "start" else local.wait()

    def pair():
        return remote(pp_ref, pp_ref, s4.at[0, 8], r4.at[0, 8], other)

    def fourth():
        collect(0, parts[0])
        for e, (sy, base, n, m) in enumerate(couplings):
            pl.when(y == sy)(functools.partial(couple, e, "start"))
        for q in range(1, len(parts)):
            collect(q, parts[q])
        for e, (sy, base, n, m) in enumerate(couplings):

            @pl.when(y != sy)
            def _():
                arrived(pp_ref.at[base : base + n], r5.at[e])

            pl.when(y == sy)(functools.partial(couple, e, "wait"))
        if couplings:
            pair().start()
        for p, (sy, i) in enumerate(panels):

            @pl.when(y != sy)
            def _():
                arrived(u_ref.at[p], ru.at[p])

        each(column, "wait")

    def handed():
        for q, ts in enumerate(parts):
            for d in range(4):
                arrived(part_x(d, ts), r4.at[q, d])
                arrived(part_z(d, ts), r4.at[q, 4 + d])
        if couplings:
            pair().wait_recv()

    def finish():
        each(scatter, "wait")
        for build in late:
            remote(*build()).wait_send()
        if couplings:
            pair().wait_send()

    stage(lambda: each(scatter, "start"))
    yield

    @stage
    def _():
        pieces()
        second_x()
        each(column, "start")

    yield
    stage(third_z)
    yield
    stage(third_x)
    yield
    stage(fourth)
    yield
    if cross:
        pl.when(jnp.logical_not(active))(handed)
    stage(finish)
    yield


def gather_sems(count, couplings):
    return [
        DMA((count, 4)),
        DMA((count,)),
        DMA((count, 4)),
        DMA((count,)),
        DMA((2, 4)),
        DMA((2, 4)),
        DMA((2, 2, 4)),
        DMA((2, 2, 4)),
        DMA((2, 9)),
        DMA((2, 9)),
        DMA((couplings, 4)),
        DMA((couplings,)),
    ]


CHILD_PANELS = ((0, 0), (0, 1), (1, 0), (1, 1))
PARENT_PANELS = ((0, 0), (1, 0), (2, 0), (3, 0), (0, 1))
PARENT_COUPLINGS = ((1, 0, 1, 0), (2, 1, 2, 0), (3, 3, 3, 0), (0, 6, 4, 1))
PAIR = {(1, 0): 0, (2, 0): 1, (2, 1): 2, (3, 0): 3, (3, 1): 4, (3, 2): 5, (4, 0): 6, (4, 1): 7, (4, 2): 8, (4, 3): 9}


def assemble_kernel(
    map_ref, child_ref, parent_ref, ginv_ref, a_ref, u2, w2, pp2,
    fr, acc, loct, u1, w1, pp1, lt, qcat, stg, hop, fin, sy, got, load_sem, tree_s, tree_r, h1s, h1r, h2s, h2r, ys, yr, *sems
):
    f, y, x, z = place()
    here = (f, y, 4 * x + z)

    loads = [
        pltpu.make_async_copy(child_ref.at[:, 0:1], fr.at[:, 0:1], load_sem.at[0]),
        pltpu.make_async_copy(child_ref.at[:, 1:12], fr.at[:, 1:12], load_sem.at[1]),
        pltpu.make_async_copy(parent_ref.at[0:2], acc.at[0:2], load_sem.at[2]),
        pltpu.make_async_copy(parent_ref.at[2:24], acc.at[2:24], load_sem.at[3]),
    ]
    for n in (0, 2, 1, 3):
        loads[n].start()

    barrier = pltpu.get_barrier_semaphore()
    greeted = []
    for dy in range(4):
        for dz in range(4):
            if dy or dz:
                greeted.append((f, ring(y, dy), 4 * x + ring(z, dz)))
    for dx in range(1, 4):
        greeted.append((f, y, 4 * ring(x, dx) + z))
    greeted.append((1 - f, y, 4 * x + z))
    for device in greeted:
        pl.semaphore_signal(barrier, inc=1, device_id=device, device_id_type=MESH)

    def turned(block):
        return block.T.reshape(TILE)

    offs = [lax.rem(map_ref[c, 16 * t + 3] - 3 + 16, 16) for c in range(2) for t in range(3)]
    residues = [lax.rem(o, 4) for o in offs]
    ranks = []
    for i in range(6):
        rank = jnp.int32(0)
        for k in range(i):
            rank = rank + (residues[k] == residues[i]).astype(jnp.int32)
        ranks.append(rank)

    def slot_of(r, s):
        slot = jnp.int32(-1)
        for i in range(6):
            slot = jnp.where((residues[i] == r) & (ranks[i] == s), i, slot)
        return slot

    loads[0].wait()
    for c in range(2):
        for t in range(3):
            loct[c, t] = turned(fr[c, 0, :, t * B : (t + 1) * B])
    pl.semaphore_wait(barrier, len(greeted))


    def tree_y(op):
        src = fr.at[:, 0, :, 0:B]
        for dy in AROUND:
            cp = remote(src, pp1, tree_s.at[0, dy], tree_r.at[0], (f, ring(y, dy), 4 * x + z))
            cp.start() if op == "start" else cp.wait_send()
        cp = pltpu.make_async_copy(src, pp1, tree_s.at[0, 0])
        cp.start() if op == "start" else cp.wait()

    def tree(axis, op):
        for d in AROUND:
            device = (f, y, 4 * ring(x, d) + z) if axis == 1 else (f, y, 4 * x + ring(z, d))
            cp = remote(pp1, pp1, tree_s.at[axis, d], tree_r.at[axis], device)
            cp.start() if op == "start" else cp.wait_send()

    def tree_wait(axis):
        remote(pp1, pp1, tree_s.at[axis, 0], tree_r.at[axis], here).wait_recv()

    root, line, floor = (y == 1) & (x == 0) & (z == 0), (x == 0) & (z == 0), z == 0

    panel1 = gather(CHILD_PANELS, 0, None, False, (), lambda i: fr.at[i, 0], lambda i: loct.at[i], u1, w1, None, sems[0:12])
    panel2a = gather(
        PARENT_PANELS, 1, f == 1, True, (), lambda i: acc.at[i], lambda i: loct.at[2 + i], u2, w2, pp2, sems[12:24]
    )
    panel2b = gather(
        PARENT_PANELS, 0, f == 0, True, PARENT_COUPLINGS, lambda i: acc.at[i], lambda i: loct.at[4 + i], u2, w2, pp2,
        sems[24:36],
    )
    next(panel1)

    @pl.when(root)
    def _():
        tree_y("start")

    loads[2].wait()

    @pl.when(f == 1)
    def _():
        for i in range(2):
            for t in range(3):
                loct[2 + i, t] = turned(acc[i, :, t * B : (t + 1) * B])

    next(panel2a)
    next(panel1)

    @pl.when(root)
    def _():
        tree_y("wait")

    @pl.when(line & jnp.logical_not(root))
    def _():
        tree_wait(0)

    @pl.when(line)
    def _():
        tree(1, "start")

    next(panel1)
    next(panel1)

    @pl.when(floor & jnp.logical_not(line))
    def _():
        tree_wait(1)

    @pl.when(floor)
    def _():
        tree(2, "start")

    next(panel1)

    @pl.when(jnp.logical_not(floor))
    def _():
        tree_wait(2)

    @pl.when(line)
    def _():
        tree(1, "wait")

    @pl.when(floor)
    def _():
        tree(2, "wait")

    for c in range(2):
        l10 = dot(pp1[c], ginv_ref[c, 0])
        lt[c] = rhs3(l10.T)
        v0 = u1[c]
        v1 = u1[2 + c] - dot(l10, v0)
        qcat[c] = rhs3(jnp.concatenate([dot(ginv_ref[c, 0], v0), dot(ginv_ref[c, 1], v1)], axis=0))
    loads[1].wait()

    def slab(dz, s, dx):
        r = ring(ring(z, dz), -y)
        slot = slot_of(r, s)
        c = (slot >= 3).astype(jnp.int32)
        t = jnp.maximum(slot - 3 * c, 0)
        m = lax.rem(x + dx - pick(offs, slot) // 4 - (y + r) // 4 + 8, 4)
        w0 = w1[0, c, m, t].reshape(B, B)
        wb = w1[0, 2 + c, m, t].reshape(B, B) - mul3(lhs3(w0), lt[c])
        full = jnp.concatenate([w0, wb], axis=1)
        return fr[c, 4 * t + m] - mul3(lhs3(full), qcat[c])

    def z_device(dz):
        return (f, y, 4 * x + ring(z, dz))

    def x_device(dx):
        return (f, y, 4 * ring(x, dx) + z)

    def first(s, h, dz, dx):
        sem = (h1s.at[s, h, dz, dx], h1r.at[s, h, dz, dx])
        rows = pl.ds(h * HALF, HALF)
        src = stg.at[s, dz, dx, rows]
        if not dx:
            return remote(src, fin.at[s, dx, dz, rows], *sem, z_device(dz))
        dst = hop.at[s, dz, dx, rows] if dz else fin.at[s, dx, dz, rows]
        return remote(src, dst, *sem, x_device(dx))

    def second(s, h, dz, dx):
        sem = (h2s.at[s, h, dz, dx], h2r.at[s, h, dz, dx])
        rows = pl.ds(h * HALF, HALF)
        return remote(hop.at[s, dz, dx, rows], fin.at[s, dx, dz, rows], *sem, z_device(dz))

    def compute(s, items):
        for dz, dx in items:
            if dz or dx:
                stg[s, dz, dx] = slab(dz, s, dx)
            else:
                fin[s, 0, 0] = slab(0, s, 0)

    def start(s, h, items):
        for dz, dx in items:
            first(s, h, dz, dx).start()

    own = [(0, 0)]
    straight = [(dz, 0) for dz in AROUND]
    rounds = [[(dz, dx) for dx in AROUND] for dz in (1, 3, 2, 0)]

    def forward(s, h, dx):
        for dz in AROUND:
            first(s, h, dz, dx).wait_recv()
            second(s, h, dz, dx).start()

    def y_copy(dy, s, h, dx):
        rows = pl.ds(h * HALF, HALF)
        sem = (ys.at[dy, s, h, dx], yr.at[dy, s, h, dx])
        return remote(sy.at[dy, s, dx, :, rows], got.at[dy, s, dx, :, rows], *sem, (f, ring(y, dy), 4 * x + z))

    home = ring(z, -y)
    child_of = [(slot_of(home, s) >= 3) for s in range(2)]

    def pass_y(s, h, dx):
        for dz in range(4):
            if dz and dx:
                second(s, h, dz, dx).wait_recv()
            elif dz or dx:
                first(s, h, dz, dx).wait_recv()
        rows = slice(h * HALF, (h + 1) * HALF)
        for dy in (1, 3, 2, 0):
            for t in range(3):
                res = jnp.where(child_of[s], residues[3 + t], residues[t])
                dz = lax.rem(z - ring(y, dy) + res + 8, 4)
                block = pick([fin[s, dx, k, rows, t * B : (t + 1) * B] for k in range(4)], dz)
                if dy:
                    sy[dy, s, dx, t, rows, :] = block
                else:
                    got[0, s, dx, t, rows, :] = block
            if dy:
                y_copy(dy, s, h, dx).start()

    compute(0, straight)
    start(0, 0, straight)
    for items in rounds:
        compute(0, items)
        start(0, 0, items)
    compute(0, own)
    start(0, 1, straight)
    for items in rounds:
        start(0, 1, items)
    pass_y(0, 0, 0)
    compute(1, straight + own)
    start(1, 0, straight)
    pass_y(0, 1, 0)
    forward(0, 0, 1)
    next(panel2a)
    compute(1, rounds[0])
    start(1, 0, rounds[0])
    forward(0, 0, 3)
    compute(1, rounds[1])
    start(1, 0, rounds[1])
    pass_y(0, 0, 1)
    forward(0, 0, 2)
    compute(1, rounds[2])
    start(1, 0, rounds[2])
    pass_y(0, 0, 3)
    compute(1, rounds[3])
    start(1, 0, rounds[3])
    start(1, 1, straight)
    for items in rounds:
        start(1, 1, items)
    pass_y(1, 0, 0)
    pass_y(0, 0, 2)
    forward(0, 1, 1)
    forward(0, 1, 3)
    pass_y(0, 1, 1)
    forward(0, 1, 2)
    pass_y(0, 1, 3)
    pass_y(1, 1, 0)
    pass_y(0, 1, 2)
    for h in range(2):
        forward(1, h, 1)
        forward(1, h, 3)
        pass_y(1, h, 1)
        forward(1, h, 2)
        if h:
            next(panel2a)
            next(panel2a)
        pass_y(1, h, 3)
        pass_y(1, h, 2)
    halves = [(s, h) for s in range(2) for h in range(2)]
    for s, h in halves:
        for dx in range(4):
            for dy in AROUND:
                y_copy(dy, s, h, dx).wait_recv()

    loads[3].wait()

    def landing(c, target):
        block, found = jnp.int32(0), jnp.bool_(False)
        for t in range(3):
            j = 16 * t + lax.rem(target - offs[3 * c + t] + 96 * 16, 16)
            hit = map_ref[c, j] == target
            block = jnp.where(hit, j, block)
            found = found | hit
        return block, found

    col_hits = [[landing(c, 32 * v + 16 * f + 4 * x + z) for v in range(3)] for c in range(2)]

    def add_row(u):
        for c in range(2):
            j, row_found = landing(c, 4 * u + y)
            dx = lax.rem(x - lax.rem(j, 16) // 4 + 4, 4)
            t_j = j // 16
            for v in range(3):
                i, col_found = col_hits[c][v]
                dy = lax.rem(y - lax.rem(i, 4) + 4, 4)
                s = jnp.minimum(pick(ranks[3 * c : 3 * c + 3], i // 16), 1)
                block = got[dy, s, dx, t_j]
                lanes = slice(v * B, (v + 1) * B)
                acc[u, :, lanes] += jnp.where(row_found & col_found, block, 0.0).T

    def add_rows(low, high):
        def step(u, _):
            add_row(u)
            return 0

        lax.fori_loop(low, high, step, 0)

    @pl.when(f == 0)
    def _():
        add_rows(0, 2)
        for i in range(2):
            for t in range(3):
                loct[4 + i, t] = turned(acc[i, :, t * B : (t + 1) * B])

    store = pltpu.make_async_copy(acc, a_ref, load_sem.at[0])
    next(panel2b)

    add_rows(2, 5)
    next(panel2b)
    next(panel2a)

    @pl.when(f == 1)
    def _():
        add_rows(0, 2)

    add_rows(5, 8)
    next(panel2b)
    next(panel2b)
    add_rows(8, 24)
    store.start()
    next(panel2b)
    next(panel2a)
    next(panel2b)
    next(panel1)
    for s, h in halves:
        for dz in range(4):
            for dx in range(4):
                if dz or dx:
                    first(s, h, dz, dx).wait_send()
                if dz and dx:
                    second(s, h, dz, dx).wait_send()
        for dx in range(4):
            for dy in AROUND:
                y_copy(dy, s, h, dx).wait_send()
    store.wait()


def assemble(block_map, children, parent, inverses):
    slab = (B, 3 * B)
    return pl.pallas_call(
        assemble_kernel,
        out_shape=(
            jax.ShapeDtypeStruct((24,) + slab, F32),
            jax.ShapeDtypeStruct((5,) + slab, F32),
            jax.ShapeDtypeStruct((2, 5, 4, 3) + TILE, F32),
            jax.ShapeDtypeStruct((10,) + TILE, F32),
        ),
        in_specs=[SMEM, ANY, ANY, VMEM],
        out_specs=(ANY, ANY, ANY, ANY),
        scratch_shapes=[
            pltpu.VMEM((2, 12) + slab, F32),
            pltpu.VMEM((24,) + slab, F32),
            pltpu.VMEM((6, 3) + TILE, F32),
            pltpu.VMEM((4,) + slab, F32),
            pltpu.VMEM((1, 4, 4, 3) + TILE, F32),
            pltpu.VMEM((2, B, B), F32),
            pltpu.VMEM((2, 3 * B, B), BF16),
            pltpu.VMEM((2, 6 * B, 3 * B), BF16),
            pltpu.VMEM((2, 4, 4) + slab, F32),
            pltpu.VMEM((2, 4, 4) + slab, F32),
            pltpu.VMEM((2, 4, 4) + slab, F32),
            pltpu.VMEM((4, 2, 4, 3, B, B), F32),
            pltpu.VMEM((4, 2, 4, 3, B, B), F32),
            DMA((4,)),
            DMA((3, 4)),
            DMA((3,)),
            DMA((2, 2, 4, 4)),
            DMA((2, 2, 4, 4)),
            DMA((2, 2, 4, 4)),
            DMA((2, 2, 4, 4)),
            DMA((4, 2, 2, 4)),
            DMA((4, 2, 2, 4)),
        ]
        + gather_sems(4, 1)
        + gather_sems(5, 1)
        + gather_sems(5, 4),
        compiler_params=pltpu.CompilerParams(
            collective_id=0, has_side_effects=True, vmem_limit_bytes=58 << 20
        ),
        name="assemble",
    )(block_map, children.reshape((2, 12) + slab), parent.reshape((24,) + slab), inverses)


def parent_kernel(a_ref, u_ref, w_ref, pp_ref, g_ref, out_ref, panel, lth, ltl, q_ref, qcat, gcat, wh, wl, pairs, own, load_sem):
    f, y, x, z = place()
    steps = range(5)
    col = 4 * x + z
    n = pl.program_id(0)

    @pl.when(n == 0)
    def _():
        loads = [
            pltpu.make_async_copy(pp_ref, pairs, load_sem.at[0]),
            pltpu.make_async_copy(u_ref, own, load_sem.at[1]),
        ]
        for cp in loads:
            cp.start()
        for cp in loads:
            cp.wait()
        for k in steps:
            for j in range(k):
                block = pairs[PAIR[k, j]].reshape(B, B)
                panel[k * B : (k + 1) * B, j * B : (j + 1) * B] = block
                panel[j * B : (j + 1) * B, k * B : (k + 1) * B] = block.T
            panel[k * B : (k + 1) * B, k * B : (k + 1) * B] = jnp.zeros((B, B), F32)
            panel[k * B : (k + 1) * B, 5 * B :] = own[k]
            gcat[k] = rhs3(g_ref[k])
        for j in range(4):
            here, later = slice(j * B, (j + 1) * B), slice((j + 1) * B, 5 * B)
            low = mul3(lhs3(panel[later, here]), gcat[j])
            high, rest = split(low.T)
            lth[here, later] = high
            ltl[here, later] = rest
            panel[later, (j + 1) * B :] -= dot(low, panel[here, (j + 1) * B :])
        for k in steps:
            q_ref[k * B : (k + 1) * B, :] = dot(g_ref[k], panel[k * B : (k + 1) * B, 5 * B :])
        qcat[...] = rhs3(q_ref[...])

    def keep(k, w):
        high, rest = split(w)
        wh[:, k * B : (k + 1) * B] = high
        wl[:, k * B : (k + 1) * B] = rest

    def left(low, high):
        return jnp.concatenate([wh[:, low:high], wh[:, low:high], wl[:, low:high]], axis=1)

    def earlier(k0, k1, j0, j1):
        rows, cols = slice(j0 * B, j1 * B), slice(k0 * B, k1 * B)
        low = jnp.concatenate([lth[rows, cols], ltl[rows, cols], lth[rows, cols]], axis=0)
        return mul3(left(j0 * B, j1 * B), low)

    raw = [w_ref[0, k, :, 0].reshape(4 * B, B) for k in steps]
    keep(0, raw[0])
    keep(1, raw[1] - earlier(1, 2, 0, 1))
    pair = jnp.concatenate([raw[2], raw[3]], axis=1) - earlier(2, 4, 0, 2)
    keep(2, pair[:, 0:B])
    keep(3, pair[:, B:] - earlier(3, 4, 2, 3))
    keep(4, raw[4] - earlier(4, 5, 0, 4))
    out = a_ref[...].reshape(4 * B, 3 * B) - mul3(left(0, 5 * B), qcat[...])
    out_ref[...] = out.reshape(4, B, 3 * B)

    @pl.when((f == 0) & (col < 5))
    def _():
        for k in steps:

            @pl.when(col == k)
            def _():
                scaled = mul3(left(k * B, (k + 1) * B), gcat[k])
                for i in range(4):
                    slot = 4 * n + i
                    row = 4 * slot + y

                    @pl.when(row > k)
                    def _():
                        out_ref[i, :, 0:B] = scaled[i * B : (i + 1) * B, :]

                    @pl.when(row == k)
                    def _():
                        out_ref[i, :, 0:B] = panel[k * B : (k + 1) * B, 5 * B : 6 * B]

    @pl.when(n == 0)
    def _():
        for k in steps:

            @pl.when(y == k % 4)
            def _():
                rows = q_ref[k * B : (k + 1) * B, :]
                done = (f == 0) & (col <= k)
                out_ref[k // 4, :, B:] = rows[:, B:]
                out_ref[k // 4, :, 0:B] = jnp.where(done, out_ref[k // 4, :, 0:B], rows[:, 0:B])


def parent_update(a, u, w, pp, inverses):
    def whole(shape):
        return pl.BlockSpec(shape, lambda n: (0,) * len(shape))

    return pl.pallas_call(
        parent_kernel,
        out_shape=jax.ShapeDtypeStruct((24, B, 3 * B), F32),
        grid=(6,),
        in_specs=[
            pl.BlockSpec((4, B, 3 * B), lambda n: (n, 0, 0)),
            ANY,
            pl.BlockSpec((1, 5, 4, 1) + TILE, lambda n: (n % 2, 0, 0, n // 2, 0, 0, 0, 0)),
            ANY,
            whole((5, B, B)),
        ],
        out_specs=pl.BlockSpec((4, B, 3 * B), lambda n: (n, 0, 0)),
        scratch_shapes=[
            pltpu.VMEM((5 * B, 8 * B), F32),
            pltpu.VMEM((5 * B, 5 * B), BF16),
            pltpu.VMEM((5 * B, 5 * B), BF16),
            pltpu.VMEM((5 * B, 3 * B), F32),
            pltpu.VMEM((15 * B, 3 * B), BF16),
            pltpu.VMEM((5, 3 * B, B), BF16),
            pltpu.VMEM((4 * B, 5 * B), BF16),
            pltpu.VMEM((4 * B, 5 * B), BF16),
            pltpu.VMEM((10,) + TILE, F32),
            pltpu.VMEM((5, B, 3 * B), F32),
            DMA((2,)),
        ],
        compiler_params=pltpu.CompilerParams(vmem_limit_bytes=62 << 20),
        name="parent_update",
    )(a, u, w, pp, inverses)


def body(child_fronts, parent_front, child_inverses, parent_inverses, block_map):
    a, u, w, pp = assemble(block_map, child_fronts, parent_front, child_inverses)
    return parent_update(a, u, w, pp, parent_inverses).reshape(parent_front.shape)


def solution(mesh):
    placed = (
        P("front", "row", "col"),
        P("row", ("front", "col")),
        P("front", None, None, None),
        P(),
        P("front", None),
    )
    return jax.shard_map(
        body, mesh=mesh, in_specs=placed, out_specs=P("row", ("front", "col")), check_vma=False
    )
```
